32 devices in a mesh: tensor: 2 (over y), expert: 16 (over z, x, core).
Axes of the slice: x: 2, y: 2, z: 4, core: 2. Of those that a mesh axis runs over, the one named last changes fastest.
Arguments:
- attn_partial: bfloat16 [2, 256, 4096], P('tensor', 'expert'), may hold values from -6 to 6
- norm_gain: float32 [4096], replicated, may hold values from 0.1 to 1.9
- expert_ids: int32 [256, 8], P('expert'), may hold values from 0 to 15, all different within a row; in each aligned block of 8 rows (0 to 7, 8 to 15, ...) at most 8 rows name the same one
- route_weights: float32 [256, 8], P('expert'), may hold values from 0.1 to 1
- gate_proj: bfloat16 [16, 4096, 1024], P('expert', None, 'tensor'), may hold values from -0.09375 to 0.09375
- up_proj: bfloat16 [16, 4096, 1024], P('expert', None, 'tensor'), may hold values from -0.09375 to 0.09375
- down_proj: bfloat16 [16, 1024, 4096], P('expert', None, 'tensor'), may hold values from -0.1875 to 0.1875
Outputs:
- combined: bfloat16 [256, 4096], P(('expert', 'tensor'))
The draws below stay inside these ranges and needn't reach their ends.
Inputs may be any that keep to these rules, and one draw needn't show every extreme that they name: `expert_ids`: each row names 8 different experts. In each aligned block of 8 rows (the rows of one device in the output's order) no expert is named by more than 8 rows, a bound that some block reaches.
All inputs are finite; a program needn't handle non-finite values.
Results may differ from the reference program's by a relative error of at most 0.025.
Values may be sent and summed in bfloat16 or wider, within the bound.
A program may use at most 64 MiB of HBM per device.

```python
import math
import jax
import jax.numpy as jnp
import numpy as np
from jax import lax

D = 4096
H = 1024
TOP = 8
QB = 128
ROWS = 8
TOKENS = 256
EXPERTS = 16
SHARDS = 2
CAP = 8
NB = 32


def block_levels(stream_key, dims, shards, smallest, largest):
    level, own = 1.0, jax.random.fold_in(stream_key, 6)
    for axis_at, shards_of in shards:
        heights = jnp.exp(jax.random.uniform(jax.random.fold_in(own, axis_at), (shards_of,), jnp.float32, smallest / len(shards), largest / len(shards)))
        level = level * jnp.repeat(heights, dims[axis_at] // shards_of).reshape([-1 if axis == axis_at else 1 for axis in range(len(dims))])
    return level


def shared_out(own_key, own, number, rows, amount, top, most, lean):
    ranking = jax.random.permutation(own_key, amount)
    packed, common = portions_of(amount, rows * top, most, lean, True), portions_of(amount, rows * top, most, lean, False)
    places = jnp.arange(amount)

    def named(sizes, turn):
        used = int((sizes > 0).sum())
        fixed = max(1, used // 4)
        shifted = fixed + (places - fixed + turn * (used - fixed)) % max(1, amount - fixed)
        return jnp.zeros((amount,), jnp.int32).at[ranking[jnp.where(places < fixed, places, shifted)]].set(jnp.asarray(sizes, jnp.int32))

    sizes = jnp.where(number % 4 == 0, named(packed, number // 4), named(common, number - number // 4 - 1))
    mixed = jax.random.permutation(jax.random.fold_in(own, 3), amount)
    giver, taker = mixed[0:amount // 2 * 2:2], mixed[1:amount // 2 * 2:2]
    margin = jnp.minimum(sizes[giver] - 1, most - sizes[taker]) // 2
    margin = jnp.where((giver == ranking[0]) | (taker == ranking[0]) | (sizes[taker] == 0), 0, jnp.maximum(margin, 0))
    shifted = jax.random.randint(jax.random.fold_in(own, 4), (amount // 2,), 0, 1 << 20) % (margin + 1)
    sizes = sizes.at[giver].add(-shifted).at[taker].add(shifted)
    items = jnp.searchsorted(jnp.cumsum(sizes), jnp.arange(rows * top), side="right").astype(jnp.int32)
    listing = items.reshape(top, rows).T
    listing = listing[jax.random.permutation(jax.random.fold_in(own, 1), rows)]
    turn = jax.random.randint(jax.random.fold_in(own, 2), (rows, 1), 0, top)
    return jnp.take_along_axis(listing, (jnp.arange(top)[None, :] + turn) % top, axis=1)


def portions_of(amount, total, most, slope, full):
    portions = [(1 << 20) // math.isqrt(standing ** slope) + 1 for standing in range(1, amount + 1)]
    largest = most if full else min(most, max(-(-total // amount), total * portions[0] // sum(portions)))
    least = 1 if total - largest >= amount - 1 else 0
    counts, rest = [largest] + [least] * (amount - 1), total - largest - least * (amount - 1)
    while rest > 0:
        candidates = [i for i in range(1, amount) if counts[i] < largest] or [i for i in range(1, amount) if counts[i] < most]
        pool, budget = sum([portions[i] for i in candidates]), rest
        for i in candidates:
            extra = min(most - counts[i], max(1, budget * portions[i] // pool), rest)
            counts[i] = counts[i] + extra
            rest = rest - extra
    return np.array(counts)


def centred(rng, dims, deviation, limit, split=(), kind=jnp.bfloat16):
    factor_of = block_levels(rng, dims, split, -0.22, 0.18) if split else 1.0
    values = jax.random.normal(rng, dims, jnp.float32) * deviation * factor_of
    return jnp.minimum(jnp.maximum(values, -limit), limit).astype(kind)


def setup_inputs(seed: int = 0) -> dict:
    streams_of = jax.random.split(jax.random.key(seed), 8)
    attn_partial = centred(streams_of[0], (SHARDS, TOKENS, D), 1.0, 6.0, ((0, 2), (1, 16)))
    norm_gain = jnp.clip(1.0 + 0.18 * jax.random.normal(streams_of[1], (D,), jnp.float32), 0.1, 1.9)
    expert_ids_keys = jax.random.split(jax.random.fold_in(streams_of[2], 1), TOKENS // ROWS)
    expert_ids_turns = jax.random.permutation(jax.random.fold_in(streams_of[2], 3), TOKENS // ROWS)
    expert_ids = jax.vmap(lambda own, number: shared_out(jax.random.fold_in(streams_of[2], 2), own, number, ROWS, EXPERTS, TOP, CAP, 2))(expert_ids_keys, expert_ids_turns).reshape((TOKENS, TOP))
    route_weights = jnp.clip(jnp.exp(math.log(1.0) - 2.3025851 * jax.random.uniform(streams_of[3], (TOKENS, TOP), jnp.float32) ** block_levels(streams_of[3], (TOKENS, TOP), ((0, 16),), -0.2, 0.2)), 0.1, 1.0)
    gate_proj = centred(streams_of[4], (EXPERTS, D, H), D ** -0.5, 0.09375, ((0, 16), (2, 2)))
    up_proj = centred(streams_of[5], (EXPERTS, D, H), D ** -0.5, 0.09375, ((0, 16), (2, 2)))
    down_proj = centred(streams_of[6], (EXPERTS, H, D), H ** -0.5, 0.1875, ((0, 16), (2, 2)))
    return dict(attn_partial=attn_partial, norm_gain=norm_gain, expert_ids=expert_ids, route_weights=route_weights, gate_proj=gate_proj, up_proj=up_proj, down_proj=down_proj)


def normalize_quantize(summed, norm_gain, block_width):
    row_count, feature_width = summed.shape
    mean_sq = lax.optimization_barrier(jnp.mean(summed * summed, axis=-1, keepdims=True))
    normed = summed * lax.rsqrt(mean_sq + 1e-06) * norm_gain
    blocks = normed.reshape(row_count, feature_width // block_width, block_width)
    scales = ((lax.optimization_barrier(jnp.max(jnp.abs(blocks), axis=-1)) + 1e-06) / 448.0).astype(jnp.bfloat16)
    values = (blocks / scales.astype(jnp.float32)[:, :, None]).astype(jnp.bfloat16)
    return (values.reshape(row_count, feature_width), scales)

def route_slots(grouped_ids, expert_total):
    labels = jnp.arange(expert_total, dtype=jnp.int32)
    member = lax.optimization_barrier(jnp.sum((grouped_ids[..., None] == labels).astype(jnp.int32), axis=-2))
    earlier = jnp.cumsum(member, axis=-2) - member
    return (member, earlier)

def reference(attn_partial, norm_gain, expert_ids, route_weights, gate_proj, up_proj, down_proj):
    summed = lax.optimization_barrier(jnp.sum(attn_partial.astype(jnp.float32), axis=0))
    token_total = summed.shape[0]
    values, scales = normalize_quantize(summed, norm_gain, QB)
    dequant = (values.astype(jnp.float32).reshape(token_total, NB, QB) * scales.astype(jnp.float32)[:, :, None]).astype(jnp.bfloat16)
    padded = jnp.concatenate([dequant.reshape(token_total, D), jnp.zeros((1, D), jnp.bfloat16)], axis=0)
    block_total = token_total // ROWS
    member, earlier = route_slots(expert_ids.reshape(block_total, ROWS, TOP), EXPERTS)
    labels = jnp.arange(EXPERTS, dtype=jnp.int32)
    pair_weight = lax.optimization_barrier(jnp.sum(jnp.where(expert_ids[..., None] == labels, route_weights[..., None], jnp.zeros((), route_weights.dtype)), axis=-2))
    pair_weight = pair_weight.reshape(block_total, ROWS, EXPERTS)
    block_index = jnp.arange(block_total, dtype=jnp.int32)[:, None, None]
    row_index = jnp.arange(ROWS, dtype=jnp.int32)[None, :, None]
    expert_index = jnp.arange(EXPERTS, dtype=jnp.int32)[None, None, :]
    shape_all = (block_total, ROWS, EXPERTS)
    target_expert = jnp.where(member > 0, jnp.broadcast_to(expert_index, shape_all), EXPERTS).astype(jnp.int32)
    target_slot = (block_index * CAP + earlier).astype(jnp.int32)
    token_index = jnp.broadcast_to(block_index * ROWS + row_index, shape_all).astype(jnp.int32)
    table = jnp.full((EXPERTS, block_total * CAP), token_total, jnp.int32)
    table = table.at[target_expert, target_slot].set(token_index, mode='drop')
    weight_table = jnp.zeros((EXPERTS, block_total * CAP), pair_weight.dtype)
    weight_table = weight_table.at[target_expert, target_slot].set(pair_weight, mode='drop')

    def one_expert(running, inputs_pair):
        slot_tokens, slot_weights, w_gate, w_up, w_down = inputs_pair
        gathered_rows = padded[slot_tokens]
        gate_act = jnp.dot(gathered_rows, w_gate, preferred_element_type=jnp.float32)
        up_act = jnp.dot(gathered_rows, w_up, preferred_element_type=jnp.float32)
        hidden = (jax.nn.silu(gate_act) * up_act).astype(jnp.bfloat16)
        expert_rows = jnp.dot(hidden, w_down, preferred_element_type=jnp.float32).astype(jnp.bfloat16)
        running = running.at[slot_tokens].add(slot_weights[:, None] * expert_rows.astype(jnp.float32))
        return (running, None)
    start_total = jnp.zeros((token_total + 1, D), jnp.float32)
    running, _ = lax.scan(one_expert, start_total, (table, weight_table, gate_proj, up_proj, down_proj))
    return running[:token_total].astype(jnp.bfloat16)
```

```python
import functools
import math

import jax
import jax.numpy as jnp
from jax import lax
from jax.experimental import pallas as pl
from jax.experimental.pallas import tpu as pltpu
from jax.sharding import PartitionSpec as P

QB = 128


def normalize_quantize(summed, norm_gain, block_width):
    row_count, feature_width = summed.shape
    mean_sq = jnp.mean(summed * summed, axis=-1, keepdims=True)
    normed = summed * lax.rsqrt(mean_sq + 1e-06) * norm_gain
    blocks = normed.reshape(row_count, feature_width // block_width, block_width)
    scales = ((jnp.max(jnp.abs(blocks), axis=-1) + 1e-06) / 448.0).astype(jnp.bfloat16)
    values = (blocks / scales.astype(jnp.float32)[:, :, None]).astype(jnp.bfloat16)
    return (values.reshape(row_count, feature_width), scales)


def route_slots(grouped_ids, expert_total):
    labels = jnp.arange(expert_total, dtype=jnp.int32)
    member = jnp.sum((grouped_ids[..., None] == labels).astype(jnp.int32), axis=-2)
    earlier = jnp.cumsum(member, axis=-2) - member
    return (member, earlier)


def place_rows(values, scales, member, earlier, capacity):
    places = jnp.arange(capacity, dtype=jnp.int32)
    chosen = (earlier[..., None] == places) & (member[..., None] > 0)
    chosen_bf = chosen.astype(jnp.bfloat16)
    send_values = jnp.einsum(
        "brec,brd->ebcd", chosen_bf, values, preferred_element_type=jnp.float32
    ).astype(jnp.bfloat16)
    send_scales = jnp.einsum(
        "brec,brn->ebcn", chosen_bf, scales, preferred_element_type=jnp.float32
    ).astype(jnp.bfloat16)
    return (send_values, send_scales)


def expert_front(values, scales, gate_matrix, up_matrix, block_width):
    row_count, feature_width = values.shape
    block_count = feature_width // block_width
    block_rows = math.gcd(row_count, 256)

    def front_block(inputs_pair):
        part_values, part_scales = inputs_pair
        pieces = part_values.reshape(block_rows, block_count, block_width).astype(jnp.float32)
        restored = (pieces * part_scales.astype(jnp.float32)[:, :, None]).astype(jnp.bfloat16)
        restored = restored.reshape(block_rows, feature_width)
        gate_act = jnp.dot(restored, gate_matrix, preferred_element_type=jnp.float32)
        up_act = jnp.dot(restored, up_matrix, preferred_element_type=jnp.float32)
        return (jax.nn.silu(gate_act) * up_act).astype(jnp.bfloat16)

    stacked = (
        values.reshape(row_count // block_rows, block_rows, feature_width),
        scales.reshape(row_count // block_rows, block_rows, block_count),
    )
    hidden = lax.map(front_block, stacked)
    return hidden.reshape(row_count, -1)


def routed_on_device(attn_partial, norm_gain, expert_ids, route_weights, gate_proj, up_proj, down_proj):
    tensor_count = lax.axis_size("tensor")
    expert_count = lax.axis_size("expert")
    tensor_index = lax.axis_index("tensor")
    group_tokens = expert_ids.shape[0]
    top_count = expert_ids.shape[1]
    row_count = group_tokens // tensor_count
    feature_width = attn_partial.shape[2]
    block_count = feature_width // QB
    capacity = max(2, (2 * row_count * top_count + expert_count - 1) // expert_count)
    gate_matrix = gate_proj[0]
    up_matrix = up_proj[0]
    down_matrix = down_proj[0]
    hidden_share = gate_matrix.shape[1]
    column_share = down_matrix.shape[1]
    own_start = tensor_index * row_count
    own_ids = lax.dynamic_slice_in_dim(expert_ids, own_start, row_count, 0)
    own_weights = lax.dynamic_slice_in_dim(route_weights, own_start, row_count, 0)
    partial_sum = attn_partial[0].astype(jnp.float32)
    summed = lax.psum(partial_sum.astype(jnp.bfloat16), "tensor").astype(jnp.float32)
    values, scales = normalize_quantize(summed, norm_gain, QB)
    group_ids = expert_ids.reshape(tensor_count, row_count, top_count)
    member, earlier = route_slots(group_ids, expert_count)
    send_values, send_scales = place_rows(
        values.reshape(tensor_count, row_count, feature_width),
        scales.reshape(tensor_count, row_count, block_count),
        member,
        earlier,
        capacity,
    )
    recv_values, recv_scales = (
        lax.all_to_all(send_values, "expert", split_axis=0, concat_axis=0, tiled=True),
        lax.all_to_all(send_scales, "expert", split_axis=0, concat_axis=0, tiled=True),
    )
    hidden = expert_front(
        recv_values.reshape(-1, feature_width),
        recv_scales.reshape(-1, block_count),
        gate_matrix,
        up_matrix,
        QB,
    )
    hidden = hidden.reshape(expert_count, tensor_count, capacity, hidden_share)
    own_member = lax.dynamic_index_in_dim(member, tensor_index, 0, keepdims=False)
    own_earlier = lax.dynamic_index_in_dim(earlier, tensor_index, 0, keepdims=False)
    slot_total = expert_count * tensor_count * capacity
    expert_sum = jnp.dot(
        lax.all_gather(hidden.reshape(slot_total, hidden_share), "tensor", axis=1, tiled=True),
        down_matrix,
        preferred_element_type=jnp.float32,
    )
    expert_rows = expert_sum.astype(jnp.bfloat16).reshape(
        expert_count, tensor_count, capacity, column_share
    )
    returned = lax.all_to_all(
        lax.all_to_all(expert_rows, "tensor", split_axis=1, concat_axis=3, tiled=True),
        "expert",
        split_axis=0,
        concat_axis=0,
        tiled=True,
    )
    returned = returned.reshape(expert_count, capacity, feature_width)
    labels = jnp.arange(expert_count, dtype=jnp.int32)
    pair_weight = jnp.sum(
        jnp.where(own_ids[..., None] == labels, own_weights[..., None], 0.0), axis=1
    )
    places = jnp.arange(capacity, dtype=jnp.int32)
    mixing = jnp.where(
        (own_earlier[..., None] == places) & (own_member[..., None] > 0),
        pair_weight[..., None],
        0.0,
    )
    combined = jnp.einsum(
        "rec,ecd->rd", mixing, returned.astype(jnp.float32), precision=lax.Precision.HIGHEST
    )
    return combined.astype(jnp.bfloat16)


LINES = 4
MESH = pl.DeviceIdType.MESH
TO_Y, TO_X, TO_CORE, TO_UP, TO_DOWN = range(5)


def dense_kernel(
    attn, gain, ids, weights, gate_hbm, up_hbm, down_hbm, out,
    rows, other, gate, up, down, hid_own, hid_in, total, core_out, core_in,
    x_keep, x_out, x_in, z_out, z_in, own_sum, swap_out, swap_in,
    load_sem, attn_sem, row_send, row_recv, hid_sem, core_sem, x_sem, z_send, z_recv, swap_sem,
):
    t = lax.axis_index("tensor")
    e = lax.axis_index("expert")
    a, b, c = e // 4, lax.rem(e // 2, 2), lax.rem(e, 2)
    group, width = attn.shape
    half = width // 2
    units = gate.shape[1]
    peers = {
        TO_Y: {"tensor": 1 - t, "expert": e},
        TO_X: {"tensor": t, "expert": e + 2 - 4 * b},
        TO_CORE: {"tensor": t, "expert": e + 1 - 2 * c},
        TO_UP: {"tensor": t, "expert": e + 4},
        TO_DOWN: {"tensor": t, "expert": e - 4},
    }

    loads = [
        pltpu.make_async_copy(source, target, load_sem.at[i])
        for i, (source, target) in enumerate(((gate_hbm, gate), (up_hbm, up), (down_hbm, down)))
    ]
    for load in loads:
        load.start()

    barrier = pltpu.get_barrier_semaphore()
    for kind in (TO_Y, TO_X, TO_CORE):
        pl.semaphore_signal(barrier, inc=1, device_id=peers[kind], device_id_type=MESH)
    for step in range(1, LINES):
        line_peer = {"tensor": t, "expert": lax.rem(e + 4 * step, 4 * LINES)}
        pl.semaphore_signal(barrier, inc=1, device_id=line_peer, device_id_type=MESH)
    pl.semaphore_wait(barrier, 2 + LINES)

    swap = pltpu.make_async_remote_copy(
        src_ref=attn, dst_ref=other, send_sem=attn_sem.at[0], recv_sem=attn_sem.at[1],
        device_id=peers[TO_Y], device_id_type=MESH,
    )
    swap.start()
    lane = lax.broadcasted_iota(jnp.int32, (group, QB), 1)
    pair_weight = jnp.zeros((group, QB), jnp.float32)
    for k in range(ids.shape[1]):
        named = ids[:, k : k + 1]
        hit = (named == lane) | (named + 4 * LINES == lane)
        pair_weight += jnp.where(hit, weights[:, k : k + 1], 0.0)
    high = pair_weight.astype(jnp.bfloat16).astype(jnp.float32)
    split_weight = jnp.where(lane < 4 * LINES, high, pair_weight - high).astype(jnp.bfloat16)
    rows[0, e, :, half:] = split_weight
    rows[1, e, :, half:] = split_weight
    swap.wait()
    summed = attn[...].astype(jnp.float32) + other[...].astype(jnp.float32)
    inverse = lax.rsqrt(jnp.mean(summed * summed, axis=-1, keepdims=True) + 1e-06)
    for block in range(width // QB):
        columns = slice(block * QB, (block + 1) * QB)
        normed = summed[:, columns] * inverse * gain[:, columns]
        largest = jnp.max(jnp.abs(normed), axis=-1, keepdims=True)
        scale = ((largest + 1e-06) / 448.0).astype(jnp.bfloat16).astype(jnp.float32)
        quantized = (normed / scale).astype(jnp.bfloat16).astype(jnp.float32)
        place = block * QB % half
        rows[block * QB // half, e, :, place : place + QB] = (quantized * scale).astype(jnp.bfloat16)

    sent = []

    def piece(kind, h, owner):
        return pltpu.make_async_remote_copy(
            src_ref=rows.at[h, owner], dst_ref=rows.at[h, owner],
            send_sem=row_send.at[kind, h, owner], recv_sem=row_recv.at[h, owner],
            device_id=peers[kind], device_id_type=MESH,
        )

    def send(kind, h, owner, when=None):
        if when is None:
            piece(kind, h, owner).start()
        else:
            pl.when(when)(lambda: piece(kind, h, owner).start())
        sent.append((kind, h, owner, when))

    def arrive(h, owner, when=None):
        if when is None:
            piece(TO_CORE, h, owner).wait_recv()
        else:
            pl.when(when)(lambda: piece(TO_CORE, h, owner).wait_recv())

    def owner_at(line, x):
        return line * 4 + x * 2 + c

    def at(distance, sign):
        line = a + sign * distance
        valid = (line >= 0) & (line < LINES)
        return jnp.clip(line, 0, LINES - 1), valid

    for h in (t, 1 - t):
        send(TO_UP, h, e, a < LINES - 1)
        send(TO_DOWN, h, e, a > 0)
        send(TO_X, h, e)
        send(TO_CORE, h, e)
    for distance in range(1, LINES + 1):
        if distance < LINES:
            for sign in (-1, 1):
                line, valid = at(distance, sign)
                owner = owner_at(line, b)
                arrive(t, owner, valid)
                if sign < 0:
                    send(TO_UP, t, owner, valid & (a < LINES - 1))
                else:
                    send(TO_DOWN, t, owner, valid & (a > 0))
                send(TO_X, t, owner, valid)
                if distance >= 2:
                    send(TO_Y, t, owner, valid)
                send(TO_CORE, t, owner, valid)
        if distance == 1:
            owner = owner_at(a, 1 - b)
            for h in (t, 1 - t):
                arrive(h, owner)
                send(TO_CORE, h, owner)
            for sign in (-1, 1):
                line, valid = at(1, sign)
                owner = owner_at(line, b)
                arrive(1 - t, owner, valid)
                send(TO_CORE, 1 - t, owner, valid)
        else:
            for sign in (-1, 1):
                line, valid = at(distance - 1, sign)
                owner = owner_at(line, 1 - b)
                arrive(t, owner, valid)
                send(TO_Y, t, owner, valid)
                send(TO_CORE, t, owner, valid)
    for distance in range(1, LINES):
        for sign in (-1, 1):
            line, valid = at(distance, sign)
            for x in (b, 1 - b) if distance >= 2 else (1 - b,):
                owner = owner_at(line, x)
                arrive(1 - t, owner, valid)
                send(TO_CORE, 1 - t, owner, valid)
    for line in range(LINES):
        for x in range(2):
            for h in range(2):
                arrive(h, line * 4 + x * 2 + 1 - c)

    loads[0].wait()
    loads[1].wait()
    near = a // 2
    parts = (1 - near, near)
    part_rows = hid_own.shape[1]
    groups = part_rows // group

    def hidden_copy(p):
        return pltpu.make_async_remote_copy(
            src_ref=hid_own.at[p], dst_ref=hid_in.at[p], send_sem=hid_sem.at[0, p],
            recv_sem=hid_sem.at[1, p], device_id=peers[TO_Y], device_id_type=MESH,
        )

    def core_copy(p):
        return pltpu.make_async_remote_copy(
            src_ref=core_out.at[p], dst_ref=core_in.at[p], send_sem=core_sem.at[0, p],
            recv_sem=core_sem.at[1, p], device_id=peers[TO_CORE], device_id_type=MESH,
        )

    def x_copy(p):
        return pltpu.make_async_remote_copy(
            src_ref=x_out.at[p], dst_ref=x_in.at[p], send_sem=x_sem.at[0, p],
            recv_sem=x_sem.at[1, p], device_id=peers[TO_X], device_id_type=MESH,
        )

    def z_copy(line):
        return pltpu.make_async_remote_copy(
            src_ref=z_out.at[line], dst_ref=z_in.at[a], send_sem=z_send.at[line],
            recv_sem=z_recv.at[a], device_id={"tensor": t, "expert": owner_at(line, b)},
            device_id_type=MESH,
        )

    def z_arrival(line):
        return pltpu.make_async_remote_copy(
            src_ref=z_out.at[line], dst_ref=z_in.at[line], send_sem=z_send.at[line],
            recv_sem=z_recv.at[line], device_id=peers[TO_X], device_id_type=MESH,
        )

    def front(p):
        first = parts[p] * groups
        left = rows[0, pl.ds(first, groups), :, :half].reshape(part_rows, half)
        right = rows[1, pl.ds(first, groups), :, :half].reshape(part_rows, half)

        def act(matrix):
            return jnp.dot(left, matrix[:half, :], preferred_element_type=jnp.float32) + jnp.dot(
                right, matrix[half:, :], preferred_element_type=jnp.float32
            )

        gate_act, up_act = act(gate), act(up)
        hid_own[p] = (gate_act / (1.0 + jnp.exp(-gate_act)) * up_act).astype(jnp.bfloat16)
        hidden_copy(p).start()

    def back(p):
        hidden_copy(p).wait_recv()
        mine = pl.ds(pl.multiple_of(t * units, units), units)
        theirs = pl.ds(pl.multiple_of((1 - t) * units, units), units)
        acc = jnp.dot(hid_own[p], down[mine, :], preferred_element_type=jnp.float32)
        acc += jnp.dot(hid_in[p], down[theirs, :], preferred_element_type=jnp.float32)
        tails = rows[0, pl.ds(parts[p] * groups, groups), :, half:].reshape(part_rows, QB)
        tail_lane = lax.broadcasted_iota(jnp.int32, (part_rows, QB), 1)
        own = (tail_lane == e) | (tail_lane == e + 4 * LINES)
        weight = jnp.sum(jnp.where(own, tails.astype(jnp.float32), 0.0), axis=-1, keepdims=True)
        total[p] = (acc * weight).reshape(groups, group, half)
        for g in range(groups // 2):
            core_out[p, g] = total[p, 2 * g + 1 - c].astype(jnp.bfloat16)
        core_copy(p).start()

    def join_cores(p):
        core_copy(p).wait_recv()
        for line in range(2):
            away = 2 * line + 1 - b
            x_out[p, line] = (total[p, 2 * away + c] + core_in[p, away].astype(jnp.float32)).astype(jnp.bfloat16)
        x_copy(p).start()
        for line in range(2):
            stay = 2 * line + b
            x_keep[p, line] = total[p, 2 * stay + c] + core_in[p, stay].astype(jnp.float32)

    def join_x(p):
        x_copy(p).wait_recv()
        for i in range(2):
            line = parts[p] * 2 + i
            joined = x_keep[p, i] + x_in[p, i].astype(jnp.float32)
            if p == 0:
                z_out[line] = joined.astype(jnp.bfloat16)
                z_copy(line).start()
            else:
                @pl.when(line == a)
                def _():
                    own_sum[...] = joined

                @pl.when(line != a)
                def _():
                    z_out[line] = joined.astype(jnp.bfloat16)
                    z_copy(line).start()

    front(0)
    front(1)
    loads[2].wait()
    back(0)
    join_cores(0)
    back(1)
    join_cores(1)
    join_x(0)
    join_x(1)
    final = own_sum[...]
    for step in range(1, LINES):
        line = lax.rem(a + step, LINES)
        z_arrival(line).wait_recv()
        final += z_in[line].astype(jnp.float32)
    top, low = final[: group // 2], final[group // 2 :]
    kept = jnp.where(t == 0, top, low)
    given = jnp.where(t == 0, low, top)
    quarter = half // 2
    swap_out[...] = jnp.concatenate([given[:, :quarter], given[:, quarter:]], axis=0).astype(jnp.bfloat16)
    swap = pltpu.make_async_remote_copy(
        src_ref=swap_out, dst_ref=swap_in, send_sem=swap_sem.at[0], recv_sem=swap_sem.at[1],
        device_id=peers[TO_Y], device_id_type=MESH,
    )
    swap.start()
    out[:, pl.ds(pl.multiple_of(t * half, half), half)] = kept.astype(jnp.bfloat16)
    for kind, h, owner, when in sent:
        if when is None:
            piece(kind, h, owner).wait_send()
        else:
            pl.when(when)(functools.partial(lambda k, i, o: piece(k, i, o).wait_send(), kind, h, owner))
    for p in range(2):
        hidden_copy(p).wait_send()
        core_copy(p).wait_send()
        x_copy(p).wait_send()
    for step in range(1, LINES):
        z_copy(lax.rem(a + step, LINES)).wait_send()
    swap.wait()
    taken = swap_in[...].astype(jnp.float32)
    taken = jnp.concatenate([taken[: group // 2], taken[group // 2 :]], axis=1)
    out[:, pl.ds(pl.multiple_of((1 - t) * half, half), half)] = taken.astype(jnp.bfloat16)


def dense_on_device(attn_partial, norm_gain, expert_ids, route_weights, gate_proj, up_proj, down_proj):
    group, width = attn_partial.shape[1:]
    experts = 4 * LINES
    half, units = width // 2, gate_proj.shape[2]
    part_rows = experts // 2 * group
    bf, f32 = jnp.bfloat16, jnp.float32
    dma = pltpu.SemaphoreType.DMA
    vmem, hbm = pl.BlockSpec(memory_space=pltpu.VMEM), pl.BlockSpec(memory_space=pl.ANY)
    return pl.pallas_call(
        dense_kernel,
        out_shape=jax.ShapeDtypeStruct((group // 2, width), bf),
        in_specs=[vmem] * 4 + [hbm] * 3,
        out_specs=vmem,
        scratch_shapes=[
            pltpu.VMEM((2, experts, group, half + QB), bf),
            pltpu.VMEM((group, width), bf),
            pltpu.VMEM(gate_proj.shape[1:], bf),
            pltpu.VMEM(up_proj.shape[1:], bf),
            pltpu.VMEM(down_proj.shape[1:], bf),
            pltpu.VMEM((2, part_rows, units), bf),
            pltpu.VMEM((2, part_rows, units), bf),
            pltpu.VMEM((2, experts // 2, group, half), f32),
            pltpu.VMEM((2, experts // 4, group, half), bf),
            pltpu.VMEM((2, experts // 4, group, half), bf),
            pltpu.VMEM((2, experts // 8, group, half), f32),
            pltpu.VMEM((2, experts // 8, group, half), bf),
            pltpu.VMEM((2, experts // 8, group, half), bf),
            pltpu.VMEM((LINES, group, half), bf),
            pltpu.VMEM((LINES, group, half), bf),
            pltpu.VMEM((group, half), f32),
            pltpu.VMEM((group, half // 2), bf),
            pltpu.VMEM((group, half // 2), bf),
            dma((3,)), dma((2,)), dma((5, 2, experts)), dma((2, experts)),
            dma((2, 2)), dma((2, 2)), dma((2, 2)), dma((LINES,)), dma((LINES,)), dma((2,)),
        ],
        compiler_params=pltpu.CompilerParams(
            collective_id=0, has_side_effects=True, vmem_limit_bytes=48 * 1024 * 1024
        ),
    )(
        attn_partial[0], norm_gain.reshape(1, width), expert_ids, route_weights,
        gate_proj[0], up_proj[0], down_proj[0],
    )


def on_device(attn_partial, norm_gain, expert_ids, route_weights, gate_proj, up_proj, down_proj):
    pairs = lax.axis_size("tensor") == 2 and lax.axis_size("expert") == 4 * LINES
    if pairs and expert_ids.shape[0] == 16 and gate_proj.shape[0] == 1:
        return dense_on_device(
            attn_partial, norm_gain, expert_ids, route_weights, gate_proj, up_proj, down_proj
        )
    return routed_on_device(
        attn_partial, norm_gain, expert_ids, route_weights, gate_proj, up_proj, down_proj
    )


def solution(mesh):
    return jax.shard_map(
        on_device,
        mesh=mesh,
        in_specs=(
            P("tensor", "expert", None),
            P(),
            P("expert", None),
            P("expert", None),
            P("expert", None, "tensor"),
            P("expert", None, "tensor"),
            P("expert", None, "tensor"),
        ),
        out_specs=P(("expert", "tensor"), None),
        check_vma=False,
    )
```

```python
import functools
import math

import jax
import jax.numpy as jnp
from jax import lax
from jax.experimental import pallas as pl
from jax.experimental.pallas import tpu as pltpu
from jax.sharding import PartitionSpec as P

QB = 128


def normalize_quantize(summed, norm_gain, block_width):
    row_count, feature_width = summed.shape
    mean_sq = jnp.mean(summed * summed, axis=-1, keepdims=True)
    normed = summed * lax.rsqrt(mean_sq + 1e-06) * norm_gain
    blocks = normed.reshape(row_count, feature_width // block_width, block_width)
    scales = ((jnp.max(jnp.abs(blocks), axis=-1) + 1e-06) / 448.0).astype(jnp.bfloat16)
    values = (blocks / scales.astype(jnp.float32)[:, :, None]).astype(jnp.bfloat16)
    return (values.reshape(row_count, feature_width), scales)


def route_slots(grouped_ids, expert_total):
    labels = jnp.arange(expert_total, dtype=jnp.int32)
    member = jnp.sum((grouped_ids[..., None] == labels).astype(jnp.int32), axis=-2)
    earlier = jnp.cumsum(member, axis=-2) - member
    return (member, earlier)


def place_rows(values, scales, member, earlier, capacity):
    places = jnp.arange(capacity, dtype=jnp.int32)
    chosen = (earlier[..., None] == places) & (member[..., None] > 0)
    chosen_bf = chosen.astype(jnp.bfloat16)
    send_values = jnp.einsum(
        "brec,brd->ebcd", chosen_bf, values, preferred_element_type=jnp.float32
    ).astype(jnp.bfloat16)
    send_scales = jnp.einsum(
        "brec,brn->ebcn", chosen_bf, scales, preferred_element_type=jnp.float32
    ).astype(jnp.bfloat16)
    return (send_values, send_scales)


def expert_front(values, scales, gate_matrix, up_matrix, block_width):
    row_count, feature_width = values.shape
    block_count = feature_width // block_width
    block_rows = math.gcd(row_count, 256)

    def front_block(inputs_pair):
        part_values, part_scales = inputs_pair
        pieces = part_values.reshape(block_rows, block_count, block_width).astype(jnp.float32)
        restored = (pieces * part_scales.astype(jnp.float32)[:, :, None]).astype(jnp.bfloat16)
        restored = restored.reshape(block_rows, feature_width)
        gate_act = jnp.dot(restored, gate_matrix, preferred_element_type=jnp.float32)
        up_act = jnp.dot(restored, up_matrix, preferred_element_type=jnp.float32)
        return (jax.nn.silu(gate_act) * up_act).astype(jnp.bfloat16)

    stacked = (
        values.reshape(row_count // block_rows, block_rows, feature_width),
        scales.reshape(row_count // block_rows, block_rows, block_count),
    )
    hidden = lax.map(front_block, stacked)
    return hidden.reshape(row_count, -1)


def routed_on_device(attn_partial, norm_gain, expert_ids, route_weights, gate_proj, up_proj, down_proj):
    tensor_count = lax.axis_size("tensor")
    expert_count = lax.axis_size("expert")
    tensor_index = lax.axis_index("tensor")
    group_tokens = expert_ids.shape[0]
    top_count = expert_ids.shape[1]
    row_count = group_tokens // tensor_count
    feature_width = attn_partial.shape[2]
    block_count = feature_width // QB
    capacity = max(2, (2 * row_count * top_count + expert_count - 1) // expert_count)
    gate_matrix = gate_proj[0]
    up_matrix = up_proj[0]
    down_matrix = down_proj[0]
    hidden_share = gate_matrix.shape[1]
    column_share = down_matrix.shape[1]
    own_start = tensor_index * row_count
    own_ids = lax.dynamic_slice_in_dim(expert_ids, own_start, row_count, 0)
    own_weights = lax.dynamic_slice_in_dim(route_weights, own_start, row_count, 0)
    partial_sum = attn_partial[0].astype(jnp.float32)
    summed = lax.psum(partial_sum.astype(jnp.bfloat16), "tensor").astype(jnp.float32)
    values, scales = normalize_quantize(summed, norm_gain, QB)
    group_ids = expert_ids.reshape(tensor_count, row_count, top_count)
    member, earlier = route_slots(group_ids, expert_count)
    send_values, send_scales = place_rows(
        values.reshape(tensor_count, row_count, feature_width),
        scales.reshape(tensor_count, row_count, block_count),
        member,
        earlier,
        capacity,
    )
    recv_values, recv_scales = (
        lax.all_to_all(send_values, "expert", split_axis=0, concat_axis=0, tiled=True),
        lax.all_to_all(send_scales, "expert", split_axis=0, concat_axis=0, tiled=True),
    )
    hidden = expert_front(
        recv_values.reshape(-1, feature_width),
        recv_scales.reshape(-1, block_count),
        gate_matrix,
        up_matrix,
        QB,
    )
    hidden = hidden.reshape(expert_count, tensor_count, capacity, hidden_share)
    own_member = lax.dynamic_index_in_dim(member, tensor_index, 0, keepdims=False)
    own_earlier = lax.dynamic_index_in_dim(earlier, tensor_index, 0, keepdims=False)
    slot_total = expert_count * tensor_count * capacity
    expert_sum = jnp.dot(
        lax.all_gather(hidden.reshape(slot_total, hidden_share), "tensor", axis=1, tiled=True),
        down_matrix,
        preferred_element_type=jnp.float32,
    )
    expert_rows = expert_sum.astype(jnp.bfloat16).reshape(
        expert_count, tensor_count, capacity, column_share
    )
    returned = lax.all_to_all(
        lax.all_to_all(expert_rows, "tensor", split_axis=1, concat_axis=3, tiled=True),
        "expert",
        split_axis=0,
        concat_axis=0,
        tiled=True,
    )
    returned = returned.reshape(expert_count, capacity, feature_width)
    labels = jnp.arange(expert_count, dtype=jnp.int32)
    pair_weight = jnp.sum(
        jnp.where(own_ids[..., None] == labels, own_weights[..., None], 0.0), axis=1
    )
    places = jnp.arange(capacity, dtype=jnp.int32)
    mixing = jnp.where(
        (own_earlier[..., None] == places) & (own_member[..., None] > 0),
        pair_weight[..., None],
        0.0,
    )
    combined = jnp.einsum(
        "rec,ecd->rd", mixing, returned.astype(jnp.float32), precision=lax.Precision.HIGHEST
    )
    return combined.astype(jnp.bfloat16)


LINES = 4
MESH = pl.DeviceIdType.MESH
TO_Y, TO_X, TO_CORE = range(3)


def dense_kernel(
    attn_hbm, gain_hbm, ids_hbm, weights_hbm, gate_hbm, up_hbm, down_hbm, out,
    attn, gain, ids, weights, table, rows, other, gate, up, down, hid_own, hid_in, total, core_out, core_in,
    x_out, x_in, z_out, z_in, swap_out, swap_in,
    load_sem, attn_sem, row_send, line_send, row_recv, hid_sem, core_sem, x_sem, z_send, z_recv, swap_sem,
):
    t = lax.axis_index("tensor")
    e = lax.axis_index("expert")
    a, b, c = e // 4, lax.rem(e // 2, 2), lax.rem(e, 2)
    group, width = attn.shape
    half = width // 2
    units = gate.shape[1]
    peers = {
        TO_Y: {"tensor": 1 - t, "expert": e},
        TO_X: {"tensor": t, "expert": e + 2 - 4 * b},
        TO_CORE: {"tensor": t, "expert": e + 1 - 2 * c},
    }

    loads = [
        pltpu.make_async_copy(source, target, load_sem.at[i])
        for i, (source, target) in enumerate((
            (attn_hbm, attn), (ids_hbm, ids), (weights_hbm, weights), (gain_hbm, gain),
            (gate_hbm, gate), (up_hbm, up), (down_hbm, down),
        ))
    ]
    for load in loads:
        load.start()

    barrier = pltpu.get_barrier_semaphore()
    for kind in (TO_Y, TO_X, TO_CORE):
        pl.semaphore_signal(barrier, inc=1, device_id=peers[kind], device_id_type=MESH)
    for step in range(1, LINES):
        line_peer = {"tensor": t, "expert": lax.rem(e + 4 * step, 4 * LINES)}
        pl.semaphore_signal(barrier, inc=1, device_id=line_peer, device_id_type=MESH)
    pl.semaphore_wait(barrier, 2 + LINES)

    swap = pltpu.make_async_remote_copy(
        src_ref=attn_hbm, dst_ref=other, send_sem=attn_sem.at[0], recv_sem=attn_sem.at[1],
        device_id=peers[TO_Y], device_id_type=MESH,
    )
    swap.start()
    experts = 4 * LINES
    for load in loads[:4]:
        load.wait()
    label = lax.broadcasted_iota(jnp.int32, (QB, group), 0)
    pair_weight = jnp.zeros((QB, group), jnp.float32)
    for k in range(ids.shape[0]):
        named = ids[k : k + 1, :]
        hit = (named == label) | (named + experts == label)
        pair_weight += jnp.where(hit, weights[k : k + 1, :], 0.0)
    high = pair_weight.astype(jnp.bfloat16).astype(jnp.float32)
    table[...] = jnp.zeros_like(table)
    table[:, :group] = jnp.where(label < experts, high, pair_weight - high)
    split_weight = table[...].T[:group].astype(jnp.bfloat16)
    rows[0, e, :, half:] = split_weight
    rows[1, e, :, half:] = split_weight
    swap.wait()
    summed = attn[...].astype(jnp.float32) + other[...].astype(jnp.float32)
    inverse = lax.rsqrt(jnp.mean(summed * summed, axis=-1, keepdims=True) + 1e-06)
    for block in range(width // QB):
        columns = slice(block * QB, (block + 1) * QB)
        normed = summed[:, columns] * inverse * gain[:, columns]
        largest = jnp.max(jnp.abs(normed), axis=-1, keepdims=True)
        scale = ((largest + 1e-06) / 448.0).astype(jnp.bfloat16).astype(jnp.float32)
        quantized = (normed / scale).astype(jnp.bfloat16).astype(jnp.float32)
        place = block * QB % half
        rows[block * QB // half, e, :, place : place + QB] = (quantized * scale).astype(jnp.bfloat16)

    sent = []

    def piece(kind, h, owner):
        return pltpu.make_async_remote_copy(
            src_ref=rows.at[h, owner], dst_ref=rows.at[h, owner],
            send_sem=row_send.at[kind, h, owner], recv_sem=row_recv.at[h, owner],
            device_id=peers[kind], device_id_type=MESH,
        )

    def send(kind, h, owner, when=None):
        if when is None:
            piece(kind, h, owner).start()
        else:
            pl.when(when)(lambda: piece(kind, h, owner).start())
        sent.append((kind, h, owner, when))

    def arrive(h, owner, when=None):
        if when is None:
            piece(TO_CORE, h, owner).wait_recv()
        else:
            pl.when(when)(lambda: piece(TO_CORE, h, owner).wait_recv())

    def owner_at(line, x):
        return line * 4 + x * 2 + c

    def at(distance, sign):
        line = a + sign * distance
        valid = (line >= 0) & (line < LINES)
        return jnp.clip(line, 0, LINES - 1), valid

    def line_piece(h, line):
        return pltpu.make_async_remote_copy(
            src_ref=rows.at[h, e], dst_ref=rows.at[h, e], send_sem=line_send.at[h, line],
            recv_sem=row_recv.at[h, e], device_id={"tensor": t, "expert": owner_at(line, b)},
            device_id_type=MESH,
        )

    def along_line(act):
        for h, distances in ((t, range(1, LINES)), (1 - t, (1,))):
            for distance in distances:
                for sign in (-1, 1):
                    line, valid = at(distance, sign)
                    pl.when(valid)(functools.partial(act, h, line))

    send(TO_X, t, e)
    send(TO_CORE, t, e)
    along_line(lambda h, line: line_piece(h, line).start())
    send(TO_X, 1 - t, e)
    send(TO_CORE, 1 - t, e)
    for distance in range(1, LINES + 2):
        if distance < LINES:
            for sign in (-1, 1):
                line, valid = at(distance, sign)
                owner = owner_at(line, b)
                arrive(t, owner, valid)
                send(TO_X, t, owner, valid)
                if distance >= 2:
                    send(TO_Y, t, owner, valid)
                send(TO_CORE, t, owner, valid)
        if distance == 1:
            owner = owner_at(a, 1 - b)
            arrive(t, owner)
            send(TO_CORE, t, owner)
        elif distance <= LINES:
            for sign in (-1, 1):
                line, valid = at(distance - 1, sign)
                owner = owner_at(line, 1 - b)
                arrive(t, owner, valid)
                send(TO_Y, t, owner, valid)
                send(TO_CORE, t, owner, valid)
    owner = owner_at(a, 1 - b)
    arrive(1 - t, owner)
    send(TO_CORE, 1 - t, owner)
    for distance in range(1, LINES):
        for sign in (-1, 1):
            line, valid = at(distance, sign)
            for x in (b, 1 - b):
                owner = owner_at(line, x)
                arrive(1 - t, owner, valid)
                send(TO_CORE, 1 - t, owner, valid)
    for line in range(LINES):
        for x in range(2):
            for h in range(2):
                arrive(h, line * 4 + x * 2 + 1 - c)

    loads[4].wait()
    loads[5].wait()
    near = a // 2
    parts = (1 - near, near)
    side = lax.rem(a, 2)
    lines = (2 - 2 * near + side, 3 - 2 * near - side, 2 * near + 1 - side, a)
    line_rows = hid_own.shape[1]
    part_rows = 2 * line_rows

    def hidden_copy(p):
        return pltpu.make_async_remote_copy(
            src_ref=hid_own.at[p], dst_ref=hid_in.at[p], send_sem=hid_sem.at[0, p],
            recv_sem=hid_sem.at[1, p], device_id=peers[TO_Y], device_id_type=MESH,
        )

    def core_copy(p):
        return pltpu.make_async_remote_copy(
            src_ref=core_out.at[p], dst_ref=core_in.at[p], send_sem=core_sem.at[0, p],
            recv_sem=core_sem.at[1, p], device_id=peers[TO_CORE], device_id_type=MESH,
        )

    def x_copy(p):
        return pltpu.make_async_remote_copy(
            src_ref=x_out.at[p], dst_ref=x_in.at[p], send_sem=x_sem.at[0, p],
            recv_sem=x_sem.at[1, p], device_id=peers[TO_X], device_id_type=MESH,
        )

    def z_copy(line):
        return pltpu.make_async_remote_copy(
            src_ref=z_out.at[line], dst_ref=z_in.at[a], send_sem=z_send.at[line],
            recv_sem=z_recv.at[a], device_id={"tensor": t, "expert": owner_at(line, b)},
            device_id_type=MESH,
        )

    def z_arrival(line):
        return pltpu.make_async_remote_copy(
            src_ref=z_out.at[line], dst_ref=z_in.at[line], send_sem=z_send.at[line],
            recv_sem=z_recv.at[line], device_id=peers[TO_X], device_id_type=MESH,
        )

    def front(p):
        left = rows[0, pl.ds(parts[p] * 8, 8), :, :half].reshape(part_rows, half)
        right = rows[1, pl.ds(parts[p] * 8, 8), :, :half].reshape(part_rows, half)

        def act(matrix):
            return jnp.dot(left, matrix[:half, :], preferred_element_type=jnp.float32) + jnp.dot(
                right, matrix[half:, :], preferred_element_type=jnp.float32
            )

        gate_act, up_act = act(gate), act(up)
        hidden = (gate_act / (1.0 + jnp.exp(-gate_act)) * up_act).astype(jnp.bfloat16)
        first = lax.rem(lines[2 * p], 2)
        hid_own[2 * p + first] = hidden[:line_rows]
        hid_own[2 * p + 1 - first] = hidden[line_rows:]
        for q in (2 * p, 2 * p + 1):
            hidden_copy(q).start()

    def back(q):
        hidden_copy(q).wait_recv()
        mine = pl.ds(pl.multiple_of(t * units, units), units)
        theirs = pl.ds(pl.multiple_of((1 - t) * units, units), units)
        acc = jnp.dot(hid_own[q], down[mine, :], preferred_element_type=jnp.float32)
        acc += jnp.dot(hid_in[q], down[theirs, :], preferred_element_type=jnp.float32)
        tails = rows[0, pl.ds(lines[q] * 4, 4), :, half:].reshape(line_rows, QB)
        tail_lane = lax.broadcasted_iota(jnp.int32, (line_rows, QB), 1)
        own = (tail_lane == e) | (tail_lane == e + experts)
        weight = jnp.sum(jnp.where(own, tails.astype(jnp.float32), 0.0), axis=-1, keepdims=True)
        total[q] = (acc * weight).reshape(4, group, half)
        for x in range(2):
            core_out[q, x] = total[q, 2 * x + 1 - c].astype(jnp.bfloat16)
        core_copy(q).start()

    def join_cores(q):
        core_copy(q).wait_recv()
        away = 1 - b
        x_out[q] = (total[q, 2 * away + c] + core_in[q, away].astype(jnp.float32)).astype(jnp.bfloat16)
        x_copy(q).start()

    def join_x(q):
        x_copy(q).wait_recv()
        joined = total[q, 2 * b + c] + core_in[q, b].astype(jnp.float32) + x_in[q].astype(jnp.float32)
        if q == LINES - 1:
            return joined
        z_out[lines[q]] = joined.astype(jnp.bfloat16)
        z_copy(lines[q]).start()

    front(0)
    front(1)
    loads[6].wait()
    back(0)
    back(1)
    join_cores(0)
    back(2)
    join_cores(1)
    join_x(0)
    back(3)
    join_cores(2)
    join_x(1)
    join_cores(3)
    join_x(2)
    final = join_x(3)
    for step in range(1, LINES):
        line = lax.rem(a + step, LINES)
        z_arrival(line).wait_recv()
        final += z_in[line].astype(jnp.float32)
    top, low = final[: group // 2], final[group // 2 :]
    kept = jnp.where(t == 0, top, low)
    given = jnp.where(t == 0, low, top)
    quarter = half // 2
    swap_out[...] = jnp.concatenate([given[:, :quarter], given[:, quarter:]], axis=0).astype(jnp.bfloat16)
    swap = pltpu.make_async_remote_copy(
        src_ref=swap_out, dst_ref=swap_in, send_sem=swap_sem.at[0], recv_sem=swap_sem.at[1],
        device_id=peers[TO_Y], device_id_type=MESH,
    )
    swap.start()
    out[:, pl.ds(pl.multiple_of(t * half, half), half)] = kept.astype(jnp.bfloat16)
    for kind, h, owner, when in sent:
        if when is None:
            piece(kind, h, owner).wait_send()
        else:
            pl.when(when)(functools.partial(lambda k, i, o: piece(k, i, o).wait_send(), kind, h, owner))
    along_line(lambda h, line: line_piece(h, line).wait_send())
    for p in range(LINES):
        hidden_copy(p).wait_send()
        core_copy(p).wait_send()
        x_copy(p).wait_send()
    for step in range(1, LINES):
        z_copy(lax.rem(a + step, LINES)).wait_send()
    swap.wait()
    taken = swap_in[...].astype(jnp.float32)
    taken = jnp.concatenate([taken[: group // 2], taken[group // 2 :]], axis=1)
    out[:, pl.ds(pl.multiple_of((1 - t) * half, half), half)] = taken.astype(jnp.bfloat16)


def dense_on_device(attn_partial, norm_gain, expert_ids, route_weights, gate_proj, up_proj, down_proj):
    group, width = attn_partial.shape[1:]
    experts = 4 * LINES
    half, units = width // 2, gate_proj.shape[2]
    line_rows = 4 * group
    bf, f32 = jnp.bfloat16, jnp.float32
    dma = pltpu.SemaphoreType.DMA
    vmem, hbm = pl.BlockSpec(memory_space=pltpu.VMEM), pl.BlockSpec(memory_space=pltpu.HBM)
    return pl.pallas_call(
        dense_kernel,
        out_shape=jax.ShapeDtypeStruct((group // 2, width), bf),
        in_specs=[hbm] * 7,
        out_specs=vmem,
        scratch_shapes=[
            pltpu.VMEM((group, width), bf),
            pltpu.VMEM((1, width), f32),
            pltpu.VMEM((expert_ids.shape[1], group), jnp.int32),
            pltpu.VMEM((expert_ids.shape[1], group), f32),
            pltpu.VMEM((QB, QB), f32),
            pltpu.VMEM((2, experts, group, half + QB), bf),
            pltpu.VMEM((group, width), bf),
            pltpu.VMEM(gate_proj.shape[1:], bf),
            pltpu.VMEM(up_proj.shape[1:], bf),
            pltpu.VMEM(down_proj.shape[1:], bf),
            pltpu.VMEM((LINES, line_rows, units), bf),
            pltpu.VMEM((LINES, line_rows, units), bf),
            pltpu.VMEM((LINES, 4, group, half), f32),
            pltpu.VMEM((LINES, 2, group, half), bf),
            pltpu.VMEM((LINES, 2, group, half), bf),
            pltpu.VMEM((LINES, group, half), bf),
            pltpu.VMEM((LINES, group, half), bf),
            pltpu.VMEM((LINES, group, half), bf),
            pltpu.VMEM((LINES, group, half), bf),
            pltpu.VMEM((group, half // 2), bf),
            pltpu.VMEM((group, half // 2), bf),
            dma((7,)), dma((2,)), dma((3, 2, experts)), dma((2, LINES)), dma((2, experts)),
            dma((2, LINES)), dma((2, LINES)), dma((2, LINES)), dma((LINES,)), dma((LINES,)), dma((2,)),
        ],
        compiler_params=pltpu.CompilerParams(
            collective_id=0, has_side_effects=True, vmem_limit_bytes=63 * 1024 * 1024
        ),
    )(
        attn_partial[0], norm_gain.reshape(1, width), expert_ids.T, route_weights.T,
        gate_proj[0], up_proj[0], down_proj[0],
    )


def on_device(attn_partial, norm_gain, expert_ids, route_weights, gate_proj, up_proj, down_proj):
    pairs = lax.axis_size("tensor") == 2 and lax.axis_size("expert") == 4 * LINES
    if pairs and expert_ids.shape[0] == 16 and gate_proj.shape[0] == 1:
        return dense_on_device(
            attn_partial, norm_gain, expert_ids, route_weights, gate_proj, up_proj, down_proj
        )
    return routed_on_device(
        attn_partial, norm_gain, expert_ids, route_weights, gate_proj, up_proj, down_proj
    )


def solution(mesh):
    return jax.shard_map(
        on_device,
        mesh=mesh,
        in_specs=(
            P("tensor", "expert", None),
            P(),
            P("expert", None),
            P("expert", None),
            P("expert", None, "tensor"),
            P("expert", None, "tensor"),
            P("expert", None, "tensor"),
        ),
        out_specs=P(("expert", "tensor"), None),
        check_vma=False,
    )
```

```python
import functools
import math

import jax
import jax.numpy as jnp
from jax import lax
from jax.experimental import pallas as pl
from jax.experimental.pallas import tpu as pltpu
from jax.sharding import PartitionSpec as P

QB = 128


def normalize_quantize(summed, norm_gain, block_width):
    row_count, feature_width = summed.shape
    mean_sq = jnp.mean(summed * summed, axis=-1, keepdims=True)
    normed = summed * lax.rsqrt(mean_sq + 1e-06) * norm_gain
    blocks = normed.reshape(row_count, feature_width // block_width, block_width)
    scales = ((jnp.max(jnp.abs(blocks), axis=-1) + 1e-06) / 448.0).astype(jnp.bfloat16)
    values = (blocks / scales.astype(jnp.float32)[:, :, None]).astype(jnp.bfloat16)
    return (values.reshape(row_count, feature_width), scales)


def route_slots(grouped_ids, expert_total):
    labels = jnp.arange(expert_total, dtype=jnp.int32)
    member = jnp.sum((grouped_ids[..., None] == labels).astype(jnp.int32), axis=-2)
    earlier = jnp.cumsum(member, axis=-2) - member
    return (member, earlier)


def place_rows(values, scales, member, earlier, capacity):
    places = jnp.arange(capacity, dtype=jnp.int32)
    chosen = (earlier[..., None] == places) & (member[..., None] > 0)
    chosen_bf = chosen.astype(jnp.bfloat16)
    send_values = jnp.einsum(
        "brec,brd->ebcd", chosen_bf, values, preferred_element_type=jnp.float32
    ).astype(jnp.bfloat16)
    send_scales = jnp.einsum(
        "brec,brn->ebcn", chosen_bf, scales, preferred_element_type=jnp.float32
    ).astype(jnp.bfloat16)
    return (send_values, send_scales)


def expert_front(values, scales, gate_matrix, up_matrix, block_width):
    row_count, feature_width = values.shape
    block_count = feature_width // block_width
    block_rows = math.gcd(row_count, 256)

    def front_block(inputs_pair):
        part_values, part_scales = inputs_pair
        pieces = part_values.reshape(block_rows, block_count, block_width).astype(jnp.float32)
        restored = (pieces * part_scales.astype(jnp.float32)[:, :, None]).astype(jnp.bfloat16)
        restored = restored.reshape(block_rows, feature_width)
        gate_act = jnp.dot(restored, gate_matrix, preferred_element_type=jnp.float32)
        up_act = jnp.dot(restored, up_matrix, preferred_element_type=jnp.float32)
        return (jax.nn.silu(gate_act) * up_act).astype(jnp.bfloat16)

    stacked = (
        values.reshape(row_count // block_rows, block_rows, feature_width),
        scales.reshape(row_count // block_rows, block_rows, block_count),
    )
    hidden = lax.map(front_block, stacked)
    return hidden.reshape(row_count, -1)


def routed_on_device(attn_partial, norm_gain, expert_ids, route_weights, gate_proj, up_proj, down_proj):
    tensor_count = lax.axis_size("tensor")
    expert_count = lax.axis_size("expert")
    tensor_index = lax.axis_index("tensor")
    group_tokens = expert_ids.shape[0]
    top_count = expert_ids.shape[1]
    row_count = group_tokens // tensor_count
    feature_width = attn_partial.shape[2]
    block_count = feature_width // QB
    capacity = max(2, (2 * row_count * top_count + expert_count - 1) // expert_count)
    gate_matrix = gate_proj[0]
    up_matrix = up_proj[0]
    down_matrix = down_proj[0]
    hidden_share = gate_matrix.shape[1]
    column_share = down_matrix.shape[1]
    own_start = tensor_index * row_count
    own_ids = lax.dynamic_slice_in_dim(expert_ids, own_start, row_count, 0)
    own_weights = lax.dynamic_slice_in_dim(route_weights, own_start, row_count, 0)
    partial_sum = attn_partial[0].astype(jnp.float32)
    summed = lax.psum(partial_sum.astype(jnp.bfloat16), "tensor").astype(jnp.float32)
    values, scales = normalize_quantize(summed, norm_gain, QB)
    group_ids = expert_ids.reshape(tensor_count, row_count, top_count)
    member, earlier = route_slots(group_ids, expert_count)
    send_values, send_scales = place_rows(
        values.reshape(tensor_count, row_count, feature_width),
        scales.reshape(tensor_count, row_count, block_count),
        member,
        earlier,
        capacity,
    )
    recv_values, recv_scales = (
        lax.all_to_all(send_values, "expert", split_axis=0, concat_axis=0, tiled=True),
        lax.all_to_all(send_scales, "expert", split_axis=0, concat_axis=0, tiled=True),
    )
    hidden = expert_front(
        recv_values.reshape(-1, feature_width),
        recv_scales.reshape(-1, block_count),
        gate_matrix,
        up_matrix,
        QB,
    )
    hidden = hidden.reshape(expert_count, tensor_count, capacity, hidden_share)
    own_member = lax.dynamic_index_in_dim(member, tensor_index, 0, keepdims=False)
    own_earlier = lax.dynamic_index_in_dim(earlier, tensor_index, 0, keepdims=False)
    slot_total = expert_count * tensor_count * capacity
    expert_sum = jnp.dot(
        lax.all_gather(hidden.reshape(slot_total, hidden_share), "tensor", axis=1, tiled=True),
        down_matrix,
        preferred_element_type=jnp.float32,
    )
    expert_rows = expert_sum.astype(jnp.bfloat16).reshape(
        expert_count, tensor_count, capacity, column_share
    )
    returned = lax.all_to_all(
        lax.all_to_all(expert_rows, "tensor", split_axis=1, concat_axis=3, tiled=True),
        "expert",
        split_axis=0,
        concat_axis=0,
        tiled=True,
    )
    returned = returned.reshape(expert_count, capacity, feature_width)
    labels = jnp.arange(expert_count, dtype=jnp.int32)
    pair_weight = jnp.sum(
        jnp.where(own_ids[..., None] == labels, own_weights[..., None], 0.0), axis=1
    )
    places = jnp.arange(capacity, dtype=jnp.int32)
    mixing = jnp.where(
        (own_earlier[..., None] == places) & (own_member[..., None] > 0),
        pair_weight[..., None],
        0.0,
    )
    combined = jnp.einsum(
        "rec,ecd->rd", mixing, returned.astype(jnp.float32), precision=lax.Precision.HIGHEST
    )
    return combined.astype(jnp.bfloat16)


LINES = 4
MESH = pl.DeviceIdType.MESH
TO_Y, TO_X, TO_CORE = range(3)


def dense_kernel(
    attn_hbm, gain_hbm, ids_hbm, weights_hbm, gate_hbm, up_hbm, down_hbm, out,
    attn, gain, ids, weights, table, rows, other, gate, up, down, gate_acc, up_acc, hid_own, hid_in, total, core_out, core_in,
    x_out, x_in, z_out, z_in, swap_out, swap_in,
    load_sem, attn_sem, row_send, line_send, row_recv, hid_sem, core_sem, x_sem, z_send, z_recv, swap_sem,
):
    t = lax.axis_index("tensor")
    e = lax.axis_index("expert")
    a, b, c = e // 4, lax.rem(e // 2, 2), lax.rem(e, 2)
    group, width = attn.shape
    half = width // 2
    units = gate.shape[1]
    peers = {
        TO_Y: {"tensor": 1 - t, "expert": e},
        TO_X: {"tensor": t, "expert": e + 2 - 4 * b},
        TO_CORE: {"tensor": t, "expert": e + 1 - 2 * c},
    }

    loads = [
        pltpu.make_async_copy(source, target, load_sem.at[i])
        for i, (source, target) in enumerate((
            (attn_hbm, attn), (ids_hbm, ids), (weights_hbm, weights), (gain_hbm, gain),
            (gate_hbm, gate), (up_hbm, up), (down_hbm, down),
        ))
    ]
    for load in loads:
        load.start()

    barrier = pltpu.get_barrier_semaphore()
    for kind in (TO_Y, TO_X, TO_CORE):
        pl.semaphore_signal(barrier, inc=1, device_id=peers[kind], device_id_type=MESH)
    for step in range(1, LINES):
        line_peer = {"tensor": t, "expert": lax.rem(e + 4 * step, 4 * LINES)}
        pl.semaphore_signal(barrier, inc=1, device_id=line_peer, device_id_type=MESH)
    pl.semaphore_wait(barrier, 2 + LINES)

    swap = pltpu.make_async_remote_copy(
        src_ref=attn_hbm, dst_ref=other, send_sem=attn_sem.at[0], recv_sem=attn_sem.at[1],
        device_id=peers[TO_Y], device_id_type=MESH,
    )
    swap.start()
    experts = 4 * LINES
    for load in loads[:4]:
        load.wait()
    label = lax.broadcasted_iota(jnp.int32, (QB, group), 0)
    pair_weight = jnp.zeros((QB, group), jnp.float32)
    for k in range(ids.shape[0]):
        named = ids[k : k + 1, :]
        hit = (named == label) | (named + experts == label)
        pair_weight += jnp.where(hit, weights[k : k + 1, :], 0.0)
    high = pair_weight.astype(jnp.bfloat16).astype(jnp.float32)
    table[...] = jnp.zeros_like(table)
    table[:, :group] = jnp.where(label < experts, high, pair_weight - high)
    split_weight = table[...].T[:group].astype(jnp.bfloat16)
    rows[0, e, :, half:] = split_weight
    rows[1, e, :, half:] = split_weight
    swap.wait()
    summed = attn[...].astype(jnp.float32) + other[...].astype(jnp.float32)
    inverse = lax.rsqrt(jnp.mean(summed * summed, axis=-1, keepdims=True) + 1e-06)
    for block in range(width // QB):
        columns = slice(block * QB, (block + 1) * QB)
        normed = summed[:, columns] * inverse * gain[:, columns]
        largest = jnp.max(jnp.abs(normed), axis=-1, keepdims=True)
        scale = ((largest + 1e-06) / 448.0).astype(jnp.bfloat16).astype(jnp.float32)
        quantized = (normed / scale).astype(jnp.bfloat16).astype(jnp.float32)
        place = block * QB % half
        rows[block * QB // half, e, :, place : place + QB] = (quantized * scale).astype(jnp.bfloat16)

    sent = []

    def piece(kind, h, owner):
        return pltpu.make_async_remote_copy(
            src_ref=rows.at[h, owner], dst_ref=rows.at[h, owner],
            send_sem=row_send.at[kind, h, owner], recv_sem=row_recv.at[h, owner],
            device_id=peers[kind], device_id_type=MESH,
        )

    def send(kind, h, owner, when=None):
        if when is None:
            piece(kind, h, owner).start()
        else:
            pl.when(when)(lambda: piece(kind, h, owner).start())
        sent.append((kind, h, owner, when))

    def arrive(h, owner, when=None):
        if when is None:
            piece(TO_CORE, h, owner).wait_recv()
        else:
            pl.when(when)(lambda: piece(TO_CORE, h, owner).wait_recv())

    def owner_at(line, x):
        return line * 4 + x * 2 + c

    def at(distance, sign):
        line = a + sign * distance
        valid = (line >= 0) & (line < LINES)
        return jnp.clip(line, 0, LINES - 1), valid

    def line_piece(h, line):
        return pltpu.make_async_remote_copy(
            src_ref=rows.at[h, e], dst_ref=rows.at[h, e], send_sem=line_send.at[h, line],
            recv_sem=row_recv.at[h, e], device_id={"tensor": t, "expert": owner_at(line, b)},
            device_id_type=MESH,
        )

    def along_line(act):
        for h, distances in ((t, range(1, LINES)), (1 - t, (1,))):
            for distance in distances:
                for sign in (-1, 1):
                    line, valid = at(distance, sign)
                    pl.when(valid)(functools.partial(act, h, line))

    send(TO_X, t, e)
    send(TO_CORE, t, e)
    pair = a + 1 - 2 * lax.rem(a, 2)
    along_line(lambda h, line: line_piece(h, line).start())
    send(TO_X, 1 - t, e)
    send(TO_CORE, 1 - t, e)
    for distance in range(1, LINES + 2):
        if distance < LINES:
            for sign in (-1, 1):
                line, valid = at(distance, sign)
                owner = owner_at(line, b)
                arrive(t, owner, valid)
                send(TO_X, t, owner, valid)
                if distance >= 2:
                    send(TO_Y, t, owner, valid)
                send(TO_CORE, t, owner, valid)
        if distance == 1:
            owner = owner_at(a, 1 - b)
            arrive(t, owner)
            send(TO_CORE, t, owner)
        elif distance <= LINES:
            for sign in (-1, 1):
                line, valid = at(distance - 1, sign)
                owner = owner_at(line, 1 - b)
                arrive(t, owner, valid)
                send(TO_Y, t, owner, valid & (line != pair))
                send(TO_CORE, t, owner, valid)
    owner = owner_at(a, 1 - b)
    arrive(1 - t, owner)
    send(TO_CORE, 1 - t, owner)
    for distance in range(1, LINES):
        for sign in (-1, 1):
            line, valid = at(distance, sign)
            owner = owner_at(line, b)
            arrive(1 - t, owner, valid)
            if distance == 1:
                send(TO_X, 1 - t, owner, valid & (line == pair))
            send(TO_CORE, 1 - t, owner, valid)
    for line in range(LINES):
        for x in range(2):
            arrive(t, line * 4 + x * 2 + 1 - c)

    def half_product(matrix, h, first, count):
        depth = pl.ds(pl.multiple_of(h * half, half), half)
        tokens = rows[h, pl.ds(first, count), :, :half].reshape(count * group, half)
        return jnp.dot(tokens, matrix[depth, :], preferred_element_type=jnp.float32)

    def far_x(distance):
        for sign in (-1, 1):
            line, valid = at(distance, sign)
            owner = owner_at(line, 1 - b)
            arrive(1 - t, owner, valid)
            send(TO_CORE, 1 - t, owner, valid)

    loads[4].wait()
    gate_acc[...] = half_product(gate, t, 0, experts)
    far_x(1)
    loads[5].wait()
    up_acc[...] = half_product(up, t, 0, experts)
    far_x(2)
    far_x(3)
    for line in range(LINES):
        for x in range(2):
            arrive(1 - t, line * 4 + x * 2 + 1 - c)

    near = a // 2
    parts = (1 - near, near)
    side = lax.rem(a, 2)
    lines = (2 - 2 * near + side, 3 - 2 * near - side, 2 * near + 1 - side, a)
    line_rows = hid_own.shape[1]
    part_rows = 2 * line_rows

    def hidden_copy(p):
        return pltpu.make_async_remote_copy(
            src_ref=hid_own.at[p], dst_ref=hid_in.at[p], send_sem=hid_sem.at[0, p],
            recv_sem=hid_sem.at[1, p], device_id=peers[TO_Y], device_id_type=MESH,
        )

    def core_copy(p):
        return pltpu.make_async_remote_copy(
            src_ref=core_out.at[p], dst_ref=core_in.at[p], send_sem=core_sem.at[0, p],
            recv_sem=core_sem.at[1, p], device_id=peers[TO_CORE], device_id_type=MESH,
        )

    def x_copy(p):
        return pltpu.make_async_remote_copy(
            src_ref=x_out.at[p], dst_ref=x_in.at[p], send_sem=x_sem.at[0, p],
            recv_sem=x_sem.at[1, p], device_id=peers[TO_X], device_id_type=MESH,
        )

    def z_copy(line):
        return pltpu.make_async_remote_copy(
            src_ref=z_out.at[line], dst_ref=z_in.at[a], send_sem=z_send.at[line],
            recv_sem=z_recv.at[a], device_id={"tensor": t, "expert": owner_at(line, b)},
            device_id_type=MESH,
        )

    def z_arrival(line):
        return pltpu.make_async_remote_copy(
            src_ref=z_out.at[line], dst_ref=z_in.at[line], send_sem=z_send.at[line],
            recv_sem=z_recv.at[line], device_id=peers[TO_X], device_id_type=MESH,
        )

    def front(p):
        span = pl.ds(pl.multiple_of(parts[p] * part_rows, part_rows), part_rows)
        gate_act = gate_acc[span, :] + half_product(gate, 1 - t, parts[p] * 8, 8)
        up_act = up_acc[span, :] + half_product(up, 1 - t, parts[p] * 8, 8)
        hidden = (gate_act / (1.0 + jnp.exp(-gate_act)) * up_act).astype(jnp.bfloat16)
        first = lax.rem(lines[2 * p], 2)
        hid_own[2 * p + first] = hidden[:line_rows]
        hid_own[2 * p + 1 - first] = hidden[line_rows:]
        for q in (2 * p, 2 * p + 1):
            hidden_copy(q).start()

    def back(q):
        hidden_copy(q).wait_recv()
        mine = pl.ds(pl.multiple_of(t * units, units), units)
        theirs = pl.ds(pl.multiple_of((1 - t) * units, units), units)
        acc = jnp.dot(hid_own[q], down[mine, :], preferred_element_type=jnp.float32)
        acc += jnp.dot(hid_in[q], down[theirs, :], preferred_element_type=jnp.float32)
        tails = rows[0, pl.ds(lines[q] * 4, 4), :, half:].reshape(line_rows, QB)
        tail_lane = lax.broadcasted_iota(jnp.int32, (line_rows, QB), 1)
        own = (tail_lane == e) | (tail_lane == e + experts)
        weight = jnp.sum(jnp.where(own, tails.astype(jnp.float32), 0.0), axis=-1, keepdims=True)
        total[q] = (acc * weight).reshape(4, group, half)
        for x in range(2):
            core_out[q, x] = total[q, 2 * x + 1 - c].astype(jnp.bfloat16)
        core_copy(q).start()

    def join_cores(q):
        core_copy(q).wait_recv()
        away = 1 - b
        x_out[q] = (total[q, 2 * away + c] + core_in[q, away].astype(jnp.float32)).astype(jnp.bfloat16)
        x_copy(q).start()

    def join_x(q):
        x_copy(q).wait_recv()
        joined = total[q, 2 * b + c] + core_in[q, b].astype(jnp.float32) + x_in[q].astype(jnp.float32)
        if q == LINES - 1:
            return joined
        z_out[lines[q]] = joined.astype(jnp.bfloat16)
        z_copy(lines[q]).start()

    front(0)
    front(1)
    loads[6].wait()
    back(0)
    back(1)
    join_cores(0)
    back(2)
    join_cores(1)
    join_x(0)
    back(3)
    join_cores(2)
    join_x(1)
    join_cores(3)
    join_x(2)
    final = join_x(3)
    for step in range(1, LINES):
        line = lax.rem(a + step, LINES)
        z_arrival(line).wait_recv()
        final += z_in[line].astype(jnp.float32)
    top, low = final[: group // 2], final[group // 2 :]
    kept = jnp.where(t == 0, top, low)
    given = jnp.where(t == 0, low, top)
    quarter = half // 2
    swap_out[...] = jnp.concatenate([given[:, :quarter], given[:, quarter:]], axis=0).astype(jnp.bfloat16)
    swap = pltpu.make_async_remote_copy(
        src_ref=swap_out, dst_ref=swap_in, send_sem=swap_sem.at[0], recv_sem=swap_sem.at[1],
        device_id=peers[TO_Y], device_id_type=MESH,
    )
    swap.start()
    out[:, pl.ds(pl.multiple_of(t * half, half), half)] = kept.astype(jnp.bfloat16)
    for kind, h, owner, when in sent:
        if when is None:
            piece(kind, h, owner).wait_send()
        else:
            pl.when(when)(functools.partial(lambda k, i, o: piece(k, i, o).wait_send(), kind, h, owner))
    along_line(lambda h, line: line_piece(h, line).wait_send())
    for p in range(LINES):
        hidden_copy(p).wait_send()
        core_copy(p).wait_send()
        x_copy(p).wait_send()
    for step in range(1, LINES):
        z_copy(lax.rem(a + step, LINES)).wait_send()
    swap.wait()
    taken = swap_in[...].astype(jnp.float32)
    taken = jnp.concatenate([taken[: group // 2], taken[group // 2 :]], axis=1)
    out[:, pl.ds(pl.multiple_of((1 - t) * half, half), half)] = taken.astype(jnp.bfloat16)


def dense_on_device(attn_partial, norm_gain, expert_ids, route_weights, gate_proj, up_proj, down_proj):
    group, width = attn_partial.shape[1:]
    experts = 4 * LINES
    half, units = width // 2, gate_proj.shape[2]
    line_rows = 4 * group
    bf, f32 = jnp.bfloat16, jnp.float32
    dma = pltpu.SemaphoreType.DMA
    vmem, hbm = pl.BlockSpec(memory_space=pltpu.VMEM), pl.BlockSpec(memory_space=pltpu.HBM)
    return pl.pallas_call(
        dense_kernel,
        out_shape=jax.ShapeDtypeStruct((group // 2, width), bf),
        in_specs=[hbm] * 7,
        out_specs=vmem,
        scratch_shapes=[
            pltpu.VMEM((group, width), bf),
            pltpu.VMEM((1, width), f32),
            pltpu.VMEM((expert_ids.shape[1], group), jnp.int32),
            pltpu.VMEM((expert_ids.shape[1], group), f32),
            pltpu.VMEM((QB, QB), f32),
            pltpu.VMEM((2, experts, group, half + QB), bf),
            pltpu.VMEM((group, width), bf),
            pltpu.VMEM(gate_proj.shape[1:], bf),
            pltpu.VMEM(up_proj.shape[1:], bf),
            pltpu.VMEM(down_proj.shape[1:], bf),
            pltpu.VMEM((LINES * line_rows, units), f32),
            pltpu.VMEM((LINES * line_rows, units), f32),
            pltpu.VMEM((LINES, line_rows, units), bf),
            pltpu.VMEM((LINES, line_rows, units), bf),
            pltpu.VMEM((LINES, 4, group, half), f32),
            pltpu.VMEM((LINES, 2, group, half), bf),
            pltpu.VMEM((LINES, 2, group, half), bf),
            pltpu.VMEM((LINES, group, half), bf),
            pltpu.VMEM((LINES, group, half), bf),
            pltpu.VMEM((LINES, group, half), bf),
            pltpu.VMEM((LINES, group, half), bf),
            pltpu.VMEM((group, half // 2), bf),
            pltpu.VMEM((group, half // 2), bf),
            dma((7,)), dma((2,)), dma((3, 2, experts)), dma((2, LINES)), dma((2, experts)),
            dma((2, LINES)), dma((2, LINES)), dma((2, LINES)), dma((LINES,)), dma((LINES,)), dma((2,)),
        ],
        compiler_params=pltpu.CompilerParams(
            collective_id=0, has_side_effects=True, vmem_limit_bytes=63 * 1024 * 1024
        ),
    )(
        attn_partial[0], norm_gain.reshape(1, width), expert_ids.T, route_weights.T,
        gate_proj[0], up_proj[0], down_proj[0],
    )


def on_device(attn_partial, norm_gain, expert_ids, route_weights, gate_proj, up_proj, down_proj):
    pairs = lax.axis_size("tensor") == 2 and lax.axis_size("expert") == 4 * LINES
    if pairs and expert_ids.shape[0] == 16 and gate_proj.shape[0] == 1:
        return dense_on_device(
            attn_partial, norm_gain, expert_ids, route_weights, gate_proj, up_proj, down_proj
        )
    return routed_on_device(
        attn_partial, norm_gain, expert_ids, route_weights, gate_proj, up_proj, down_proj
    )


def solution(mesh):
    return jax.shard_map(
        on_device,
        mesh=mesh,
        in_specs=(
            P("tensor", "expert", None),
            P(),
            P("expert", None),
            P("expert", None),
            P("expert", None, "tensor"),
            P("expert", None, "tensor"),
            P("expert", None, "tensor"),
        ),
        out_specs=P(("expert", "tensor"), None),
        check_vma=False,
    )
```

```python
import functools
import math

import jax
import jax.numpy as jnp
from jax import lax
from jax.experimental import pallas as pl
from jax.experimental.pallas import tpu as pltpu
from jax.sharding import PartitionSpec as P

QB = 128


def normalize_quantize(summed, norm_gain, block_width):
    row_count, feature_width = summed.shape
    mean_sq = jnp.mean(summed * summed, axis=-1, keepdims=True)
    normed = summed * lax.rsqrt(mean_sq + 1e-06) * norm_gain
    blocks = normed.reshape(row_count, feature_width // block_width, block_width)
    scales = ((jnp.max(jnp.abs(blocks), axis=-1) + 1e-06) / 448.0).astype(jnp.bfloat16)
    values = (blocks / scales.astype(jnp.float32)[:, :, None]).astype(jnp.bfloat16)
    return (values.reshape(row_count, feature_width), scales)


def route_slots(grouped_ids, expert_total):
    labels = jnp.arange(expert_total, dtype=jnp.int32)
    member = jnp.sum((grouped_ids[..., None] == labels).astype(jnp.int32), axis=-2)
    earlier = jnp.cumsum(member, axis=-2) - member
    return (member, earlier)


def place_rows(values, scales, member, earlier, capacity):
    places = jnp.arange(capacity, dtype=jnp.int32)
    chosen = (earlier[..., None] == places) & (member[..., None] > 0)
    chosen_bf = chosen.astype(jnp.bfloat16)
    send_values = jnp.einsum(
        "brec,brd->ebcd", chosen_bf, values, preferred_element_type=jnp.float32
    ).astype(jnp.bfloat16)
    send_scales = jnp.einsum(
        "brec,brn->ebcn", chosen_bf, scales, preferred_element_type=jnp.float32
    ).astype(jnp.bfloat16)
    return (send_values, send_scales)


def expert_front(values, scales, gate_matrix, up_matrix, block_width):
    row_count, feature_width = values.shape
    block_count = feature_width // block_width
    block_rows = math.gcd(row_count, 256)

    def front_block(inputs_pair):
        part_values, part_scales = inputs_pair
        pieces = part_values.reshape(block_rows, block_count, block_width).astype(jnp.float32)
        restored = (pieces * part_scales.astype(jnp.float32)[:, :, None]).astype(jnp.bfloat16)
        restored = restored.reshape(block_rows, feature_width)
        gate_act = jnp.dot(restored, gate_matrix, preferred_element_type=jnp.float32)
        up_act = jnp.dot(restored, up_matrix, preferred_element_type=jnp.float32)
        return (jax.nn.silu(gate_act) * up_act).astype(jnp.bfloat16)

    stacked = (
        values.reshape(row_count // block_rows, block_rows, feature_width),
        scales.reshape(row_count // block_rows, block_rows, block_count),
    )
    hidden = lax.map(front_block, stacked)
    return hidden.reshape(row_count, -1)


def routed_on_device(attn_partial, norm_gain, expert_ids, route_weights, gate_proj, up_proj, down_proj):
    tensor_count = lax.axis_size("tensor")
    expert_count = lax.axis_size("expert")
    tensor_index = lax.axis_index("tensor")
    group_tokens = expert_ids.shape[0]
    top_count = expert_ids.shape[1]
    row_count = group_tokens // tensor_count
    feature_width = attn_partial.shape[2]
    block_count = feature_width // QB
    capacity = max(2, (2 * row_count * top_count + expert_count - 1) // expert_count)
    gate_matrix = gate_proj[0]
    up_matrix = up_proj[0]
    down_matrix = down_proj[0]
    hidden_share = gate_matrix.shape[1]
    column_share = down_matrix.shape[1]
    own_start = tensor_index * row_count
    own_ids = lax.dynamic_slice_in_dim(expert_ids, own_start, row_count, 0)
    own_weights = lax.dynamic_slice_in_dim(route_weights, own_start, row_count, 0)
    partial_sum = attn_partial[0].astype(jnp.float32)
    summed = lax.psum(partial_sum.astype(jnp.bfloat16), "tensor").astype(jnp.float32)
    values, scales = normalize_quantize(summed, norm_gain, QB)
    group_ids = expert_ids.reshape(tensor_count, row_count, top_count)
    member, earlier = route_slots(group_ids, expert_count)
    send_values, send_scales = place_rows(
        values.reshape(tensor_count, row_count, feature_width),
        scales.reshape(tensor_count, row_count, block_count),
        member,
        earlier,
        capacity,
    )
    recv_values, recv_scales = (
        lax.all_to_all(send_values, "expert", split_axis=0, concat_axis=0, tiled=True),
        lax.all_to_all(send_scales, "expert", split_axis=0, concat_axis=0, tiled=True),
    )
    hidden = expert_front(
        recv_values.reshape(-1, feature_width),
        recv_scales.reshape(-1, block_count),
        gate_matrix,
        up_matrix,
        QB,
    )
    hidden = hidden.reshape(expert_count, tensor_count, capacity, hidden_share)
    own_member = lax.dynamic_index_in_dim(member, tensor_index, 0, keepdims=False)
    own_earlier = lax.dynamic_index_in_dim(earlier, tensor_index, 0, keepdims=False)
    slot_total = expert_count * tensor_count * capacity
    expert_sum = jnp.dot(
        lax.all_gather(hidden.reshape(slot_total, hidden_share), "tensor", axis=1, tiled=True),
        down_matrix,
        preferred_element_type=jnp.float32,
    )
    expert_rows = expert_sum.astype(jnp.bfloat16).reshape(
        expert_count, tensor_count, capacity, column_share
    )
    returned = lax.all_to_all(
        lax.all_to_all(expert_rows, "tensor", split_axis=1, concat_axis=3, tiled=True),
        "expert",
        split_axis=0,
        concat_axis=0,
        tiled=True,
    )
    returned = returned.reshape(expert_count, capacity, feature_width)
    labels = jnp.arange(expert_count, dtype=jnp.int32)
    pair_weight = jnp.sum(
        jnp.where(own_ids[..., None] == labels, own_weights[..., None], 0.0), axis=1
    )
    places = jnp.arange(capacity, dtype=jnp.int32)
    mixing = jnp.where(
        (own_earlier[..., None] == places) & (own_member[..., None] > 0),
        pair_weight[..., None],
        0.0,
    )
    combined = jnp.einsum(
        "rec,ecd->rd", mixing, returned.astype(jnp.float32), precision=lax.Precision.HIGHEST
    )
    return combined.astype(jnp.bfloat16)


LINES = 4
MESH = pl.DeviceIdType.MESH
TO_Y, TO_X, TO_CORE, TO_UP, TO_DOWN = range(5)


def dense_kernel(
    attn_hbm, gain_hbm, ids_hbm, weights_hbm, gate_hbm, up_hbm, down_hbm, out,
    attn, gain, ids, weights, table, rows, other, gate, up, down, gate_acc, up_acc, hid_own, hid_in, total, core_out, core_in,
    x_out, x_in, z_out, z_in, swap_out, swap_in,
    load_sem, attn_sem, row_send, row_recv, hid_sem, core_sem, x_sem, z_send, z_recv, swap_sem,
):
    t = lax.axis_index("tensor")
    e = lax.axis_index("expert")
    a, b, c = e // 4, lax.rem(e // 2, 2), lax.rem(e, 2)
    group, width = attn.shape
    half = width // 2
    units = gate.shape[1]
    peers = {
        TO_Y: {"tensor": 1 - t, "expert": e},
        TO_X: {"tensor": t, "expert": e + 2 - 4 * b},
        TO_CORE: {"tensor": t, "expert": e + 1 - 2 * c},
        TO_UP: {"tensor": t, "expert": e + 4},
        TO_DOWN: {"tensor": t, "expert": e - 4},
    }

    loads = [
        pltpu.make_async_copy(source, target, load_sem.at[i])
        for i, (source, target) in enumerate((
            (attn_hbm, attn), (ids_hbm, ids), (weights_hbm, weights), (gain_hbm, gain),
            (gate_hbm, gate), (up_hbm, up), (down_hbm, down),
        ))
    ]
    for load in loads:
        load.start()

    barrier = pltpu.get_barrier_semaphore()
    for kind in (TO_Y, TO_X, TO_CORE):
        pl.semaphore_signal(barrier, inc=1, device_id=peers[kind], device_id_type=MESH)
    for step in range(1, LINES):
        line_peer = {"tensor": t, "expert": lax.rem(e + 4 * step, 4 * LINES)}
        pl.semaphore_signal(barrier, inc=1, device_id=line_peer, device_id_type=MESH)
    pl.semaphore_wait(barrier, 2 + LINES)

    swap = pltpu.make_async_remote_copy(
        src_ref=attn_hbm, dst_ref=other, send_sem=attn_sem.at[0], recv_sem=attn_sem.at[1],
        device_id=peers[TO_Y], device_id_type=MESH,
    )
    swap.start()
    experts = 4 * LINES
    for load in loads[:4]:
        load.wait()
    label = lax.broadcasted_iota(jnp.int32, (QB, group), 0)
    pair_weight = jnp.zeros((QB, group), jnp.float32)
    for k in range(ids.shape[0]):
        named = ids[k : k + 1, :]
        hit = (named == label) | (named + experts == label)
        pair_weight += jnp.where(hit, weights[k : k + 1, :], 0.0)
    high = pair_weight.astype(jnp.bfloat16).astype(jnp.float32)
    table[...] = jnp.zeros_like(table)
    table[:, :group] = jnp.where(label < experts, high, pair_weight - high)
    split_weight = table[...].T[:group].astype(jnp.bfloat16)
    rows[0, e, :, half:] = split_weight
    rows[1, e, :, half:] = split_weight
    swap.wait()
    summed = attn[...].astype(jnp.float32) + other[...].astype(jnp.float32)
    inverse = lax.rsqrt(jnp.mean(summed * summed, axis=-1, keepdims=True) + 1e-06)
    for block in range(width // QB):
        columns = slice(block * QB, (block + 1) * QB)
        normed = summed[:, columns] * inverse * gain[:, columns]
        largest = jnp.max(jnp.abs(normed), axis=-1, keepdims=True)
        scale = ((largest + 1e-06) / 448.0).astype(jnp.bfloat16).astype(jnp.float32)
        quantized = (normed / scale).astype(jnp.bfloat16).astype(jnp.float32)
        place = block * QB % half
        rows[block * QB // half, e, :, place : place + QB] = (quantized * scale).astype(jnp.bfloat16)

    sent = []

    def piece(kind, h, owner):
        return pltpu.make_async_remote_copy(
            src_ref=rows.at[h, owner], dst_ref=rows.at[h, owner],
            send_sem=row_send.at[kind, h, owner], recv_sem=row_recv.at[h, owner],
            device_id=peers[kind], device_id_type=MESH,
        )

    def send(kind, h, owner, when=None):
        if when is None:
            piece(kind, h, owner).start()
        else:
            pl.when(when)(lambda: piece(kind, h, owner).start())
        sent.append((kind, h, owner, when))

    def arrive(h, owner, when=None):
        if when is None:
            piece(TO_CORE, h, owner).wait_recv()
        else:
            pl.when(when)(lambda: piece(TO_CORE, h, owner).wait_recv())

    def owner_at(line, x):
        return line * 4 + x * 2 + c

    def at(distance, sign):
        line = a + sign * distance
        valid = (line >= 0) & (line < LINES)
        return jnp.clip(line, 0, LINES - 1), valid

    upper, lower = a < LINES - 1, a > 0
    send(TO_UP, t, e, upper)
    send(TO_DOWN, t, e, lower)
    send(TO_X, t, e)
    send(TO_CORE, t, e)
    for distance in range(1, LINES + 1):
        if distance < LINES:
            for sign in (-1, 1):
                line, valid = at(distance, sign)
                owner = owner_at(line, b)
                arrive(t, owner, valid)
                if sign < 0:
                    send(TO_UP, t, owner, valid & upper)
                else:
                    send(TO_DOWN, t, owner, valid & lower)
                send(TO_X, t, owner, valid)
                if distance >= 2:
                    send(TO_Y, t, owner, valid)
                send(TO_CORE, t, owner, valid)
        if distance == 1:
            owner = owner_at(a, 1 - b)
            arrive(t, owner)
            send(TO_CORE, t, owner)
            send(TO_UP, 1 - t, e, upper)
            send(TO_DOWN, 1 - t, e, lower)
            send(TO_CORE, 1 - t, e)
        else:
            for sign in (-1, 1):
                line, valid = at(distance - 1, sign)
                owner = owner_at(line, 1 - b)
                arrive(t, owner, valid)
                send(TO_Y, t, owner, valid)
                send(TO_CORE, t, owner, valid)
        if distance == 2:
            send(TO_X, 1 - t, e)
    owner = owner_at(a, 1 - b)
    arrive(1 - t, owner)
    send(TO_CORE, 1 - t, owner)
    for distance in range(1, LINES):
        for sign in (-1, 1):
            line, valid = at(distance, sign)
            owner = owner_at(line, b)
            arrive(1 - t, owner, valid)
            send(TO_CORE, 1 - t, owner, valid)

    def half_product(matrix, h, first, count):
        depth = pl.ds(pl.multiple_of(h * half, half), half)
        tokens = rows[h, pl.ds(first, count), :, :half].reshape(count * group, half)
        return jnp.dot(tokens, matrix[depth, :], preferred_element_type=jnp.float32)

    def far_x(distance):
        for sign in (-1, 1):
            line, valid = at(distance, sign)
            owner = owner_at(line, 1 - b)
            arrive(1 - t, owner, valid)
            send(TO_CORE, 1 - t, owner, valid)

    far_x(1)
    for line in range(LINES):
        for x in range(2):
            arrive(t, line * 4 + x * 2 + 1 - c)
    loads[4].wait()
    gate_acc[...] = half_product(gate, t, 0, experts)
    far_x(2)
    loads[5].wait()
    up_acc[...] = half_product(up, t, 0, experts)
    far_x(3)
    for line in range(LINES):
        for x in range(2):
            arrive(1 - t, line * 4 + x * 2 + 1 - c)

    near = a // 2
    parts = (1 - near, near)
    side = lax.rem(a, 2)
    lines = (2 - 2 * near + side, 3 - 2 * near - side, 2 * near + 1 - side, a)
    line_rows = hid_own.shape[1]
    part_rows = 2 * line_rows

    def hidden_copy(p):
        return pltpu.make_async_remote_copy(
            src_ref=hid_own.at[p], dst_ref=hid_in.at[p], send_sem=hid_sem.at[0, p],
            recv_sem=hid_sem.at[1, p], device_id=peers[TO_Y], device_id_type=MESH,
        )

    def core_copy(p):
        return pltpu.make_async_remote_copy(
            src_ref=core_out.at[p], dst_ref=core_in.at[p], send_sem=core_sem.at[0, p],
            recv_sem=core_sem.at[1, p], device_id=peers[TO_CORE], device_id_type=MESH,
        )

    def x_copy(p):
        return pltpu.make_async_remote_copy(
            src_ref=x_out.at[p], dst_ref=x_in.at[p], send_sem=x_sem.at[0, p],
            recv_sem=x_sem.at[1, p], device_id=peers[TO_X], device_id_type=MESH,
        )

    def z_copy(line):
        return pltpu.make_async_remote_copy(
            src_ref=z_out.at[line], dst_ref=z_in.at[a], send_sem=z_send.at[line],
            recv_sem=z_recv.at[a], device_id={"tensor": t, "expert": owner_at(line, b)},
            device_id_type=MESH,
        )

    def z_arrival(line):
        return pltpu.make_async_remote_copy(
            src_ref=z_out.at[line], dst_ref=z_in.at[line], send_sem=z_send.at[line],
            recv_sem=z_recv.at[line], device_id=peers[TO_X], device_id_type=MESH,
        )

    def front(p):
        span = pl.ds(pl.multiple_of(parts[p] * part_rows, part_rows), part_rows)
        gate_act = gate_acc[span, :] + half_product(gate, 1 - t, parts[p] * 8, 8)
        up_act = up_acc[span, :] + half_product(up, 1 - t, parts[p] * 8, 8)
        hidden = (gate_act / (1.0 + jnp.exp(-gate_act)) * up_act).astype(jnp.bfloat16)
        first = lax.rem(lines[2 * p], 2)
        hid_own[2 * p + first] = hidden[:line_rows]
        hid_own[2 * p + 1 - first] = hidden[line_rows:]
        hidden_copy(p).start()

    def back(q):
        hidden_copy(q).wait_recv()
        if q < 2:
            hidden_copy(q + 2).start()
        mine = pl.ds(pl.multiple_of(t * units, units), units)
        theirs = pl.ds(pl.multiple_of((1 - t) * units, units), units)
        acc = jnp.dot(hid_own[q], down[mine, :], preferred_element_type=jnp.float32)
        acc += jnp.dot(hid_in[q], down[theirs, :], preferred_element_type=jnp.float32)
        tails = rows[0, pl.ds(lines[q] * 4, 4), :, half:].reshape(line_rows, QB)
        tail_lane = lax.broadcasted_iota(jnp.int32, (line_rows, QB), 1)
        own = (tail_lane == e) | (tail_lane == e + experts)
        weight = jnp.sum(jnp.where(own, tails.astype(jnp.float32), 0.0), axis=-1, keepdims=True)
        total[q] = (acc * weight).reshape(4, group, half)
        for x in range(2):
            core_out[q, x] = total[q, 2 * x + 1 - c].astype(jnp.bfloat16)
        core_copy(q).start()

    def join_cores(q):
        core_copy(q).wait_recv()
        away = 1 - b
        x_out[q] = (total[q, 2 * away + c] + core_in[q, away].astype(jnp.float32)).astype(jnp.bfloat16)
        x_copy(q).start()

    def join_x(q):
        x_copy(q).wait_recv()
        joined = total[q, 2 * b + c] + core_in[q, b].astype(jnp.float32) + x_in[q].astype(jnp.float32)
        if q == LINES - 1:
            return joined
        z_out[lines[q]] = joined.astype(jnp.bfloat16)
        z_copy(lines[q]).start()

    front(0)
    front(1)
    loads[6].wait()
    back(0)
    back(1)
    join_cores(0)
    back(2)
    join_cores(1)
    join_x(0)
    back(3)
    join_cores(2)
    join_x(1)
    join_cores(3)
    join_x(2)
    final = join_x(3)
    for step in range(1, LINES):
        line = lax.rem(a + step, LINES)
        z_arrival(line).wait_recv()
        final += z_in[line].astype(jnp.float32)
    top, low = final[: group // 2], final[group // 2 :]
    kept = jnp.where(t == 0, top, low)
    given = jnp.where(t == 0, low, top)
    quarter = half // 2
    swap_out[...] = jnp.concatenate([given[:, :quarter], given[:, quarter:]], axis=0).astype(jnp.bfloat16)
    swap = pltpu.make_async_remote_copy(
        src_ref=swap_out, dst_ref=swap_in, send_sem=swap_sem.at[0], recv_sem=swap_sem.at[1],
        device_id=peers[TO_Y], device_id_type=MESH,
    )
    swap.start()
    out[:, pl.ds(pl.multiple_of(t * half, half), half)] = kept.astype(jnp.bfloat16)
    for kind, h, owner, when in sent:
        if when is None:
            piece(kind, h, owner).wait_send()
        else:
            pl.when(when)(functools.partial(lambda k, i, o: piece(k, i, o).wait_send(), kind, h, owner))
    for p in range(LINES):
        hidden_copy(p).wait_send()
        core_copy(p).wait_send()
        x_copy(p).wait_send()
    for step in range(1, LINES):
        z_copy(lax.rem(a + step, LINES)).wait_send()
    swap.wait()
    taken = swap_in[...].astype(jnp.float32)
    taken = jnp.concatenate([taken[: group // 2], taken[group // 2 :]], axis=1)
    out[:, pl.ds(pl.multiple_of((1 - t) * half, half), half)] = taken.astype(jnp.bfloat16)


def dense_on_device(attn_partial, norm_gain, expert_ids, route_weights, gate_proj, up_proj, down_proj):
    group, width = attn_partial.shape[1:]
    experts = 4 * LINES
    half, units = width // 2, gate_proj.shape[2]
    line_rows = 4 * group
    bf, f32 = jnp.bfloat16, jnp.float32
    dma = pltpu.SemaphoreType.DMA
    vmem, hbm = pl.BlockSpec(memory_space=pltpu.VMEM), pl.BlockSpec(memory_space=pltpu.HBM)
    return pl.pallas_call(
        dense_kernel,
        out_shape=jax.ShapeDtypeStruct((group // 2, width), bf),
        in_specs=[hbm] * 7,
        out_specs=vmem,
        scratch_shapes=[
            pltpu.VMEM((group, width), bf),
            pltpu.VMEM((1, width), f32),
            pltpu.VMEM((expert_ids.shape[1], group), jnp.int32),
            pltpu.VMEM((expert_ids.shape[1], group), f32),
            pltpu.VMEM((QB, QB), f32),
            pltpu.VMEM((2, experts, group, half + QB), bf),
            pltpu.VMEM((group, width), bf),
            pltpu.VMEM(gate_proj.shape[1:], bf),
            pltpu.VMEM(up_proj.shape[1:], bf),
            pltpu.VMEM(down_proj.shape[1:], bf),
            pltpu.VMEM((LINES * line_rows, units), f32),
            pltpu.VMEM((LINES * line_rows, units), f32),
            pltpu.VMEM((LINES, line_rows, units), bf),
            pltpu.VMEM((LINES, line_rows, units), bf),
            pltpu.VMEM((LINES, 4, group, half), f32),
            pltpu.VMEM((LINES, 2, group, half), bf),
            pltpu.VMEM((LINES, 2, group, half), bf),
            pltpu.VMEM((LINES, group, half), bf),
            pltpu.VMEM((LINES, group, half), bf),
            pltpu.VMEM((LINES, group, half), bf),
            pltpu.VMEM((LINES, group, half), bf),
            pltpu.VMEM((group, half // 2), bf),
            pltpu.VMEM((group, half // 2), bf),
            dma((7,)), dma((2,)), dma((5, 2, experts)), dma((2, experts)),
            dma((2, LINES)), dma((2, LINES)), dma((2, LINES)), dma((LINES,)), dma((LINES,)), dma((2,)),
        ],
        compiler_params=pltpu.CompilerParams(
            collective_id=0, has_side_effects=True, vmem_limit_bytes=63 * 1024 * 1024
        ),
    )(
        attn_partial[0], norm_gain.reshape(1, width), expert_ids.T, route_weights.T,
        gate_proj[0], up_proj[0], down_proj[0],
    )


def on_device(attn_partial, norm_gain, expert_ids, route_weights, gate_proj, up_proj, down_proj):
    pairs = lax.axis_size("tensor") == 2 and lax.axis_size("expert") == 4 * LINES
    if pairs and expert_ids.shape[0] == 16 and gate_proj.shape[0] == 1:
        return dense_on_device(
            attn_partial, norm_gain, expert_ids, route_weights, gate_proj, up_proj, down_proj
        )
    return routed_on_device(
        attn_partial, norm_gain, expert_ids, route_weights, gate_proj, up_proj, down_proj
    )


def solution(mesh):
    return jax.shard_map(
        on_device,
        mesh=mesh,
        in_specs=(
            P("tensor", "expert", None),
            P(),
            P("expert", None),
            P("expert", None),
            P("expert", None, "tensor"),
            P("expert", None, "tensor"),
            P("expert", None, "tensor"),
        ),
        out_specs=P(("expert", "tensor"), None),
        check_vma=False,
    )
```
